256 devices in a mesh: src: 8 (over x, core), tgt: 32 (over y, z).
Axes of the slice: x: 4, y: 4, z: 8, core: 2. Of those that a mesh axis runs over, the one named last changes fastest.
Arguments:
- source_embed: bfloat16 [16384, 256], P(('src', 'tgt'))
- source_links: int32 [16384, 8], P(('src', 'tgt')), may hold values from 0 to 2047
- source_degree: int32 [16384], P(('src', 'tgt')), may hold values from 1 to 8
- target_embed: bfloat16 [32768, 256], P('tgt')
- target_links: int32 [32768, 8], P('tgt'), may hold values from 0 to 1023
- target_degree: int32 [32768], P('tgt'), may hold values from 1 to 8
- w_self: bfloat16 [256, 256], replicated, may hold values from -0.375 to 0.375
- w_neigh: bfloat16 [256, 256], replicated, may hold values from -0.375 to 0.375
- cand_blocks: int32 [128, 32], P('src'), may hold values from 0 to 255, all different within a row; in each aligned block of 16 rows (0 to 15, 16 to 31, ...) at most 4 rows name the same one
- probe_pairs: int32 [16384, 16], P('src'), may hold values from 0 to 4095
Outputs:
- plan_scores: float32 [16384, 16], P(('src', 'tgt'))
The draws below stay inside these ranges and needn't reach their ends.
Inputs may be any that keep to these rules, and one draw needn't show every extreme that they name: `source_links`: A neighbour index within the source entity's group of 2048 entities. `target_links`: A neighbour index within the target entity's block of 1024 entities. Only the first source_degree entries of a row count. Only the first target_degree entries of a row count. `cand_blocks`: the blocks of a row are distinct; within each aligned block of 16 rows (one group) no target block is named by more than 4 rows, and some target block is named by exactly 4; every target block is named by some row. `probe_pairs`: p names candidate block p // 128 of the row's source block and the target at offset p mod 128 in it.
All inputs are finite; a program needn't handle non-finite values.
Results may differ from the reference program's by a relative error of at most 0.0018.
Values may be sent and summed in bfloat16 or wider, within the bound.
A program may use at most 64 MiB of HBM per device.

```python
import math
import jax
import jax.numpy as jnp
import numpy as np
from jax import lax

D = 256
BLK = 128
CAND = 32
MOST = 4
KMAX = 8
QRY = 16
SWEEPS = 4
T_DEV = 1024
R_GRP = 2048
NS = 16384
NT = 32768
R_BLK = 16
C_BLK = 256


def draw_source_embed(key, part):
    first, second = jax.random.split(jax.random.fold_in(key, 11))
    base = jnp.clip(jax.random.normal(first, (NS, D), jnp.float32), -4.0, 4.0)
    spread = jnp.exp(jax.random.uniform(second, (NS, 1), jnp.float32, math.log(0.6), math.log(1.7)))
    return (base * spread).astype(jnp.bfloat16)


def draw_target_embed(key, part):
    first, second = jax.random.split(jax.random.fold_in(key, 23))
    base = jnp.clip(jax.random.normal(first, (NT, D), jnp.float32), -4.0, 4.0)
    spread = jnp.exp(jax.random.uniform(second, (NT, 1), jnp.float32, math.log(0.6), math.log(1.7)))
    return (base * spread).astype(jnp.bfloat16)


def set_ends(entries, rng, least, largest):
    longest = entries.shape.index(max(entries.shape))
    spots = []
    for shift in (0, 1):
        where = [jax.random.randint(jax.random.fold_in(rng, axis), (), 0, length) for axis, length in enumerate(entries.shape)]
        where[longest] = (where[longest] + shift) % entries.shape[longest]
        spots.append(tuple(where))
    return entries.at[spots[0]].set(least).at[spots[1]].set(largest)


def deal_out(rng, own, number, rows, amount, top, most, slope):
    order = jax.random.permutation(rng, amount)
    crowded, ordinary = shares(amount, rows * top, most, slope, True), shares(amount, rows * top, most, slope, False)
    places = jnp.arange(amount)

    def named(lengths, turn):
        used = int((lengths > 0).sum())
        fixed = max(1, used // 4)
        passed = fixed + (places - fixed + turn * (used - fixed)) % max(1, amount - fixed)
        return jnp.zeros((amount,), jnp.int32).at[order[jnp.where(places < fixed, places, passed)]].set(jnp.asarray(lengths, jnp.int32))

    lengths = jnp.where(number % 4 == 0, named(crowded, number // 4), named(ordinary, number - number // 4 - 1))
    mixed = jax.random.permutation(jax.random.fold_in(own, 3), amount)
    giver, taker = mixed[0:amount // 2 * 2:2], mixed[1:amount // 2 * 2:2]
    room = jnp.minimum(lengths[giver] - 1, most - lengths[taker]) // 2
    room = jnp.where((giver == order[0]) | (taker == order[0]) | (lengths[taker] == 0), 0, jnp.maximum(room, 0))
    passed = jax.random.randint(jax.random.fold_in(own, 4), (amount // 2,), 0, 1 << 20) % (room + 1)
    lengths = lengths.at[giver].add(-passed).at[taker].add(passed)
    members = jnp.searchsorted(jnp.cumsum(lengths), jnp.arange(rows * top), side="right").astype(jnp.int32)
    table = members.reshape(top, rows).T
    table = table[jax.random.permutation(jax.random.fold_in(own, 1), rows)]
    turn = jax.random.randint(jax.random.fold_in(own, 2), (rows, 1), 0, top)
    return jnp.take_along_axis(table, (jnp.arange(top)[None, :] + turn) % top, axis=1)


def shares(number_of, total, limit, skew, full):
    loads = [(1 << 20) // math.isqrt(rank ** skew) + 1 for rank in range(1, number_of + 1)]
    largest = limit if full else min(limit, max(-(-total // number_of), total * loads[0] // sum(loads)))
    least = 1 if total - largest >= number_of - 1 else 0
    holding, spare = [largest] + [least] * (number_of - 1), total - largest - least * (number_of - 1)
    while spare > 0:
        free = [i for i in range(1, number_of) if holding[i] < largest] or [i for i in range(1, number_of) if holding[i] < limit]
        pool, left = sum([loads[i] for i in free]), spare
        for i in free:
            more = min(limit - holding[i], max(1, left * loads[i] // pool), spare)
            holding[i] = holding[i] + more
            spare = spare - more
    return np.array(holding)


def centred(key, extent, width, most, kind=jnp.bfloat16):
    array = jax.random.normal(key, extent, jnp.float32) * width
    return jnp.minimum(jnp.maximum(array, -most), most).astype(kind)


def setup_inputs(seed: int = 0) -> dict:
    arg_keys = jax.random.split(jax.random.key(seed), 11)
    source_embed = draw_source_embed(jax.random.fold_in(arg_keys[10], 71), 0)
    source_links = set_ends(jax.random.randint(arg_keys[1], (NS, KMAX), 0, R_GRP), jax.random.fold_in(arg_keys[1], 1), 0, R_GRP - 1).astype(jnp.int32)
    source_degree = set_ends(jax.random.randint(arg_keys[2], (NS,), 1, KMAX + 1), jax.random.fold_in(arg_keys[2], 1), 1, KMAX).astype(jnp.int32)
    target_embed = draw_target_embed(jax.random.fold_in(arg_keys[10], 71), 0)
    target_links = set_ends(jax.random.randint(arg_keys[4], (NT, KMAX), 0, T_DEV), jax.random.fold_in(arg_keys[4], 1), 0, T_DEV - 1).astype(jnp.int32)
    target_degree = set_ends(jax.random.randint(arg_keys[5], (NT,), 1, KMAX + 1), jax.random.fold_in(arg_keys[5], 1), 1, KMAX).astype(jnp.int32)
    w_self = centred(arg_keys[6], (D, D), D ** -0.5, 0.375)
    w_neigh = centred(arg_keys[7], (D, D), D ** -0.5, 0.375)
    cand_blocks_keys = jax.random.split(jax.random.fold_in(arg_keys[8], 1), (NS // BLK) // R_BLK)
    cand_blocks_turns = jax.random.permutation(jax.random.fold_in(arg_keys[8], 3), (NS // BLK) // R_BLK)
    cand_blocks = jax.vmap(lambda own, number: deal_out(jax.random.fold_in(arg_keys[8], 2), own, number, R_BLK, C_BLK, CAND, MOST, 2))(cand_blocks_keys, cand_blocks_turns).reshape((NS // BLK, CAND))
    probe_pairs = set_ends(jax.random.randint(arg_keys[9], (NS, QRY), 0, CAND * BLK), jax.random.fold_in(arg_keys[9], 1), 0, (CAND * BLK) - 1).astype(jnp.int32)
    return dict(source_embed=source_embed, source_links=source_links, source_degree=source_degree, target_embed=target_embed, target_links=target_links, target_degree=target_degree, w_self=w_self, w_neigh=w_neigh, cand_blocks=cand_blocks, probe_pairs=probe_pairs)


def aggregate(table, links, degree, own, w_self, w_neigh):
    total = jnp.zeros(own.shape, jnp.float32)
    for slot in range(KMAX):
        picked = jnp.take(table, links[:, slot], axis=0).astype(jnp.float32)
        total = total + jnp.where((slot < degree)[:, None], picked, 0.0)
    mean_rows = (total / degree[:, None].astype(jnp.float32)).astype(jnp.bfloat16)
    mixed = jnp.dot(own, w_self, preferred_element_type=jnp.float32) + jnp.dot(mean_rows, w_neigh, preferred_element_type=jnp.float32)
    return mixed.astype(jnp.bfloat16)

def reference(source_embed, source_links, source_degree, target_embed, target_links, target_degree, w_self, w_neigh, cand_blocks, probe_pairs):
    source_base = jnp.arange(NS, dtype=jnp.int32) // R_GRP * R_GRP
    target_base = jnp.arange(NT, dtype=jnp.int32) // T_DEV * T_DEV
    source_h = aggregate(source_embed, source_links + source_base[:, None], source_degree, source_embed, w_self, w_neigh)
    target_h = aggregate(target_embed, target_links + target_base[:, None], target_degree, target_embed, w_self, w_neigh)
    row_h = source_h.reshape(NS // BLK, BLK, D)
    col_h = target_h.reshape(C_BLK, BLK, D)
    scale = 3.0 / math.sqrt(D)

    def block_scores(items):
        block_rows, blocks = items
        picked = jnp.take(col_h, blocks, axis=0).astype(jnp.float32)
        return jnp.einsum('ad,kbd->akb', block_rows.astype(jnp.float32), picked, precision=lax.Precision.HIGHEST) * scale
    scores = lax.map(block_scores, (row_h, cand_blocks))
    column_potential = jnp.zeros((C_BLK, BLK), jnp.float32)
    log_ratio = math.log(NS / NT)
    flat_ids = cand_blocks.reshape(-1)
    row_potential = jnp.zeros((NS // BLK, BLK), jnp.float32)
    for sweep in range(SWEEPS):

        def row_pass(items):
            block_scores_now, blocks = items
            shifted = block_scores_now + jnp.take(column_potential, blocks, axis=0)[None, :, :]
            return -jax.nn.logsumexp(shifted, axis=(1, 2))
        row_potential = lax.map(row_pass, (scores, cand_blocks))

        def max_pass(items):
            block_scores_now, row_part = items
            return lax.optimization_barrier(jnp.max(block_scores_now + row_part[:, None, None], axis=0))
        part_max = lax.map(max_pass, (scores, row_potential))
        highest = jax.ops.segment_max(part_max.reshape(-1, BLK), flat_ids, num_segments=C_BLK)

        def sum_pass(items):
            block_scores_now, blocks, row_part = items
            shifted = block_scores_now + row_part[:, None, None] - jnp.take(highest, blocks, axis=0)[None, :, :]
            return lax.optimization_barrier(jnp.sum(jnp.exp(shifted), axis=0))
        part_sum = lax.map(sum_pass, (scores, cand_blocks, row_potential))
        totals = jax.ops.segment_sum(part_sum.reshape(-1, BLK), flat_ids, num_segments=C_BLK)
        column_potential = log_ratio - (highest + jnp.log(totals))
    rows_all = jnp.arange(NS, dtype=jnp.int32)
    block_of = rows_all // BLK
    inner = rows_all % BLK
    which = probe_pairs // BLK
    offset = probe_pairs % BLK
    target_block = cand_blocks[block_of[:, None], which]
    picked = scores[block_of[:, None], inner[:, None], which, offset]
    return picked + row_potential[block_of, inner][:, None] + column_potential[target_block, offset] + math.log(CAND * BLK)
```

```python
import functools
import math

import jax
import jax.numpy as jnp
from jax import lax
from jax.experimental import pallas as pl
from jax.experimental.pallas import tpu as pltpu
from jax.sharding import PartitionSpec as P

D = 256
BLK = 128
CAND = 32
MOST = 4
QRY = 16
SWEEPS = 4
KMAX = 8
NY, NZ = 4, 8
NSRC, NTGT = 8, 32
ROWS = 64
R_BLK = 16
C_LOC = 8
SLOTS = C_LOC * MOST
A_ROWS = 48
B_ROWS = 16
WIDE = 256
NEG = -1e30
FLOOR = -1e29
SCALE = 3.0 / math.sqrt(D)
MESH = pl.DeviceIdType.MESH
BF = jnp.bfloat16
F32 = jnp.float32


def far_first():
    offs = [(dy, dz) for dy in range(NY) for dz in range(NZ) if (dy, dz) != (0, 0)]
    dist = lambda o: min(o[0], NY - o[0]) + min(o[1], NZ - o[1])
    return sorted(offs, key=lambda o: (-dist(o), o))


Z_FAR = (4, 3, 5, 2, 6, 1, 7)
Z_NEAR = (1, 7, 2, 6, 3, 5, 4)
Y_FAR = (2, 1, 3)


def sinkhorn_kernel(
    srow_ref, place_ref, x_ref, sl_ref, t_ref, tl_ref, ws_ref, wn_ref, tab_ref, pp_ref,
    out_ref,
    iota_ref, big_x, xt_ref, lk_ref, at_ref, ht_ref, tt_ref, att_ref, th_ref,
    s_ref, e_ref, wb_ref, rx_ref, cx_ref, top_ref, r0_ref, u_ref, sid_ref, g_ref, pk_ref,
    fs_ref, fr_ref,
    a_send, a_recv, b_send, b_recv, ya_send, ya_recv, zb_send, zb_recv, lk_send, lk_recv,
    r_send, r_recv, c_send, c_recv, f_send, f_recv,
):
    s = lax.axis_index("src")
    t = lax.axis_index("tgt")
    y = t // NZ
    z = lax.rem(t, NZ)
    tgt_peers = [lax.rem(y + dy, NY) * NZ + lax.rem(z + dz, NZ) for dy, dz in far_first()]
    sx = s // 2
    score = lax.rem(s, 2)
    src_peers = [
        lax.rem(sx + dx, 4) * 2 + (score if same else 1 - score)
        for dx, same in ((2, False), (2, True), (1, False), (3, False), (1, True), (3, True), (0, False))
    ]

    barrier = pltpu.get_barrier_semaphore()
    for p in tgt_peers:
        pl.semaphore_signal(barrier, inc=1, device_id=(s, p), device_id_type=MESH)
    for p in src_peers:
        pl.semaphore_signal(barrier, inc=1, device_id=(p, t), device_id_type=MESH)

    tile_rows = lax.broadcasted_iota(jnp.int32, (WIDE // 16, 16, BLK), 0) * 16
    tile_rows = tile_rows + lax.broadcasted_iota(jnp.int32, (WIDE // 16, 16, BLK), 1)
    iota_ref[...] = tile_rows.astype(F32).astype(BF)
    lane8 = lax.broadcasted_iota(jnp.int32, (KMAX, BLK), 1)
    big_x[pl.ds(t * ROWS, ROWS), :] = x_ref[...]
    lk_ref[t] = jnp.where((lane8 // ROWS) == lax.rem(t, 2), sl_ref[...], 0)
    g_ref[SLOTS] = jnp.zeros((QRY, BLK), F32)

    pl.semaphore_wait(barrier, NTGT - 1 + NSRC - 1)

    def push(src, dst, ssem, rsem, dev):
        pltpu.make_async_remote_copy(
            src_ref=src, dst_ref=dst, send_sem=ssem, recv_sem=rsem, device_id=dev, device_id_type=MESH
        ).start()

    def drain(ref, sem):
        pltpu.make_async_copy(ref, ref, sem).wait()

    def part_a(d):
        return big_x.at[pl.ds(d * ROWS, A_ROWS)]

    def part_b(d):
        return big_x.at[pl.ds(d * ROWS + A_ROWS, B_ROWS)]

    def at_yz(dy, dz):
        return lax.rem(y + dy + NY, NY) * NZ + lax.rem(z + dz + NZ, NZ)

    for k in Z_FAR:
        push(part_a(t), part_a(t), a_send, a_recv.at[k], (s, at_yz(0, k)))
    for j in Y_FAR:
        push(part_b(t), part_b(t), b_send, b_recv.at[j], (s, at_yz(j, 0)))
    for p in tgt_peers:
        push(lk_ref.at[t], lk_ref.at[t], lk_send, lk_recv, (s, p))
    for j in Y_FAR:
        push(part_a(t), part_a(t), ya_send, ya_recv, (s, at_yz(j, 0)))
    for k in Z_FAR:
        push(part_b(t), part_b(t), zb_send, zb_recv, (s, at_yz(0, k)))

    ws_t = ws_ref[...].T
    wn_t = wn_ref[...].T
    for chunk in range(4):
        tt_ref[:, chunk * WIDE : (chunk + 1) * WIDE] = t_ref[chunk * WIDE : (chunk + 1) * WIDE, :].T

    for j in Y_FAR[::-1]:
        drain(part_b(t), b_recv.at[j])
        d = at_yz(-j, 0)
        for k in Z_FAR:
            push(part_b(d), part_b(d), zb_send, zb_recv, (s, at_yz(0, k)))
    for k in Z_NEAR:
        drain(part_a(t), a_recv.at[k])
        d = at_yz(0, -k)
        for j in Y_FAR:
            push(part_a(d), part_a(d), ya_send, ya_recv, (s, at_yz(j, 0)))

    def build(links, chunks, put):
        def body(q, _):
            base = (q * WIDE).astype(F32)
            near = jnp.clip(links - base, -1.0, float(WIDE))
            total = jnp.zeros((WIDE // 16, 16, BLK), BF)
            for k in range(KMAX):
                row = jnp.broadcast_to(near[k : k + 1, :], (16, BLK)).astype(BF)
                total = total + jnp.where(row[None] == iota_ref[...], 1.0, 0.0).astype(BF)
            put(q, total.reshape(WIDE, BLK))
            return 0

        lax.fori_loop(0, chunks, body, 0)

    def encode(table_t, adjacency, own_t, degree):
        total = jnp.dot(table_t, adjacency, preferred_element_type=F32)
        mean = (total / degree).astype(BF)
        mixed = jnp.dot(ws_t, own_t, preferred_element_type=F32) + jnp.dot(
            wn_t, mean, preferred_element_type=F32
        )
        return mixed.astype(BF)

    for chunk in range(4):
        cols = slice(chunk * WIDE, (chunk + 1) * WIDE)
        links = tl_ref[:, cols]
        degree = jnp.sum((links >= 0).astype(F32), axis=0, keepdims=True)
        for half in range(2):
            def put(q, value, half=half):
                att_ref[pl.ds(q * WIDE, WIDE), half * BLK : (half + 1) * BLK] = value

            build(links[:, half * BLK : (half + 1) * BLK].astype(F32), 4, put)
        coded = encode(tt_ref[...], att_ref[...], tt_ref[:, cols], degree).T
        th_ref[2 * chunk] = coded[:BLK]
        th_ref[2 * chunk + 1] = coded[BLK:]

    drain(lk_ref.at[pl.ds(0, NTGT - 1)], lk_recv)

    def group_links(block):
        return lk_ref[2 * block] + lk_ref[2 * block + 1]

    def build_pair(pair, _):
        for half in range(2):
            def put(q, value, half=half):
                at_ref[pair, pl.ds(q * WIDE, WIDE), half * BLK : (half + 1) * BLK] = value

            build(group_links(2 * pair + half).astype(F32), 8, put)
        return 0

    lax.fori_loop(0, 8, build_pair, 0)

    drain(big_x.at[pl.ds(0, 24 * A_ROWS)], ya_recv)
    drain(big_x.at[pl.ds(0, 28 * B_ROWS)], zb_recv)
    for chunk in range(8):
        xt_ref[chunk] = big_x[chunk * WIDE : (chunk + 1) * WIDE, :].T

    def encode_pair(pair, _):
        links = jnp.concatenate([group_links(2 * pair), group_links(2 * pair + 1)], axis=1)
        degree = jnp.sum((links >= 0).astype(F32), axis=0, keepdims=True)
        total = jnp.zeros((D, WIDE), F32)
        for q in range(8):
            total = total + jnp.dot(
                xt_ref[q], at_ref[pair, q * WIDE : (q + 1) * WIDE, :], preferred_element_type=F32
            )
        mean = (total / degree).astype(BF)
        mixed = jnp.dot(ws_t, xt_ref[pair], preferred_element_type=F32) + jnp.dot(
            wn_t, mean, preferred_element_type=F32
        )
        coded = mixed.astype(BF)
        ht_ref[2 * pair] = coded[:, :BLK]
        ht_ref[2 * pair + 1] = coded[:, BLK:]
        return 0

    lax.fori_loop(0, 8, encode_pair, 0)

    block_id = lax.broadcasted_iota(jnp.int32, (R_BLK, BLK), 0)
    lane = lax.broadcasted_iota(jnp.int32, (BLK, BLK), 1)
    neg16 = jnp.full((R_BLK, BLK), NEG, F32)

    def score_block(c, best):
        for m in range(MOST):
            r = srow_ref[c * MOST + m]
            bias = jnp.where(r < 0, NEG, 0.0)
            raw = jnp.dot(th_ref[c], ht_ref[jnp.maximum(r, 0)], preferred_element_type=F32)
            raw = raw * SCALE + bias
            s_ref[c * MOST + m] = raw
            best = jnp.maximum(best, jnp.where(block_id == r, jnp.max(raw, axis=0, keepdims=True), NEG))
        return best

    top = lax.fori_loop(0, C_LOC, score_block, neg16)
    top_ref[...] = top

    def first_rows(c, total):
        for m in range(MOST):
            r = srow_ref[c * MOST + m]
            high = top_ref[pl.ds(jnp.maximum(r, 0), 1), :]
            part = jnp.sum(jnp.exp(s_ref[c * MOST + m] - high), axis=0, keepdims=True)
            total = total + jnp.where(block_id == r, part, 0.0)
        return total

    total = lax.fori_loop(0, C_LOC, first_rows, jnp.zeros((R_BLK, BLK), F32))
    rx_ref[0, t] = jnp.where(total > 0.0, top + jnp.log(total), NEG)

    def send_rows(sweep):
        for p in tgt_peers:
            push(rx_ref.at[sweep, t], rx_ref.at[sweep, t], r_send.at[sweep], r_recv.at[sweep], (s, p))

    def await_rows(sweep):
        drain(rx_ref.at[sweep, pl.ds(0, NTGT - 1)], r_recv.at[sweep])
        return rx_ref[sweep]

    def send_cols(sweep):
        for p in src_peers:
            push(cx_ref.at[sweep, s], cx_ref.at[sweep, s], c_send.at[sweep], c_recv.at[sweep], (p, t))

    def await_cols(sweep):
        drain(cx_ref.at[sweep, pl.ds(0, NSRC - 1)], c_recv.at[sweep])
        return cx_ref[sweep]

    send_rows(0)

    def probe_slots(block, _):
        table = jnp.broadcast_to(tab_ref[block], (8, BLK))
        for half in range(2):
            rows = slice(half * 8, half * 8 + 8)
            which = pp_ref[block, rows, :] // BLK
            sid_ref[block, rows, :] = jnp.take_along_axis(table, which, axis=1)
        return 0

    lax.fori_loop(0, R_BLK, probe_slots, 0)

    def pick(slot, _):
        r = jnp.maximum(srow_ref[slot], 0)
        for half in range(2):
            rows = slice(half * 8, half * 8 + 8)
            offset = lax.rem(pp_ref[r, rows, :], BLK)
            strip, inner = offset // 8, lax.rem(offset, 8)
            value = jnp.zeros((8, BLK), F32)
            for k in range(BLK // 8):
                got = jnp.take_along_axis(s_ref[slot, k * 8 : k * 8 + 8, :], inner, axis=0)
                value = jnp.where(strip == k, got, value)
            g_ref[slot, rows, :] = jnp.where(sid_ref[r, rows, :] == slot, value, 0.0)
        return 0

    lax.fori_loop(0, SLOTS, pick, 0)

    def merge(block, _):
        total = jnp.zeros((QRY, BLK), F32)
        for c in range(C_LOC):
            total = total + g_ref[place_ref[block * C_LOC + c]]
        pk_ref[block] = total
        return 0

    lax.fori_loop(0, R_BLK, merge, 0)

    parts = await_rows(0)
    high = jnp.max(parts, axis=0)
    r0 = -(high + jnp.log(jnp.sum(jnp.exp(parts - high[None]), axis=0)))
    r0_ref[...] = r0

    def first_cols(c, carry):
        tops, sums = carry
        shifted = [
            s_ref[c * MOST + m] + r0_ref[pl.ds(jnp.maximum(srow_ref[c * MOST + m], 0), 1), :]
            for m in range(MOST)
        ]
        high = functools.reduce(jnp.maximum, shifted)
        high = jnp.maximum(jnp.max(high, axis=1, keepdims=True), FLOOR)
        total = jnp.zeros((BLK, BLK), F32)
        for m in range(MOST):
            e = jnp.exp(shifted[m] - high)
            e_ref[c * MOST + m] = e
            total = total + e
        total = jnp.sum(total, axis=1, keepdims=True)
        return jnp.where(lane == c, high, tops), jnp.where(lane == c, total, sums)

    zero_tile = jnp.zeros((BLK, BLK), F32)
    tops, sums = lax.fori_loop(0, C_LOC, first_cols, (zero_tile, zero_tile))
    tops = tops.T[:C_LOC]
    sums = sums.T[:C_LOC]
    cx_ref[0, s] = jnp.where(sums > 0.0, tops + jnp.log(sums), NEG)
    send_cols(0)
    parts = await_cols(0)
    high = jnp.max(parts, axis=0)
    share = R_BLK * BLK * NSRC / (C_LOC * BLK * NTGT)
    c0 = math.log(share) - (high + jnp.log(jnp.sum(jnp.exp(parts - high[None]), axis=0)))
    factor = jnp.exp(tops + c0)

    def spread(weights):
        upright = jnp.concatenate([weights, jnp.zeros((BLK - C_LOC, BLK), F32)], axis=0).T
        for c in range(C_LOC):
            wb_ref[c] = jnp.broadcast_to(upright[:, c : c + 1], (BLK, BLK))

    def sweep_body(sweep, carry):
        _, col_scale = carry
        spread(factor * col_scale)

        def rows_of(c, total):
            for m in range(MOST):
                part = jnp.sum(e_ref[c * MOST + m] * wb_ref[c], axis=0, keepdims=True)
                total = total + jnp.where(block_id == srow_ref[c * MOST + m], part, 0.0)
            return total

        rx_ref[sweep, t] = lax.fori_loop(0, C_LOC, rows_of, jnp.zeros((R_BLK, BLK), F32))
        send_rows(sweep)
        row_scale = 1.0 / jnp.sum(await_rows(sweep), axis=0)
        u_ref[...] = row_scale

        def cols_of(c, sums):
            total = jnp.zeros((BLK, BLK), F32)
            for m in range(MOST):
                r = jnp.maximum(srow_ref[c * MOST + m], 0)
                total = total + e_ref[c * MOST + m] * u_ref[pl.ds(r, 1), :]
            return jnp.where(lane == c, jnp.sum(total, axis=1, keepdims=True), sums)

        sums = lax.fori_loop(0, C_LOC, cols_of, zero_tile).T[:C_LOC]
        cx_ref[sweep, s] = sums * factor
        send_cols(sweep)
        return row_scale, share / jnp.sum(await_cols(sweep), axis=0)

    row_scale, col_scale = lax.fori_loop(
        1, SWEEPS, sweep_body, (jnp.ones((R_BLK, BLK), F32), jnp.ones((C_LOC, BLK), F32))
    )
    row_pot = r0 + jnp.log(row_scale)
    col_pot = c0 + jnp.log(col_scale) + math.log(CAND * BLK)
    u_ref[...] = row_pot
    top_ref[:C_LOC, :] = col_pot
    lane8 = lax.broadcasted_iota(jnp.int32, (8, BLK), 1)

    def finish(block, _):
        done = []
        for half in range(2):
            rows = slice(half * 8, half * 8 + 8)
            sid = sid_ref[block, rows, :]
            offset = lax.rem(pp_ref[block, rows, :], BLK)
            owner = sid // MOST
            value = jnp.zeros((8, BLK), F32)
            for c in range(C_LOC):
                strip = jnp.broadcast_to(top_ref[c : c + 1, :], (8, BLK))
                value = jnp.where(owner == c, jnp.take_along_axis(strip, offset, axis=1), value)
            value = value + pk_ref[block, rows, :] + u_ref[pl.ds(block, 1), :]
            done.append(jnp.where(sid >= 0, value, 0.0))
        low, high = done
        fs_ref[2 * block] = jnp.where(lane8 < ROWS, low, pltpu.roll(high, ROWS, 1))
        fs_ref[2 * block + 1] = jnp.where(lane8 < ROWS, pltpu.roll(low, ROWS, 1), high)
        return 0

    lax.fori_loop(0, R_BLK, finish, 0)
    for p in tgt_peers:
        push(fs_ref.at[p], fr_ref.at[t], f_send, f_recv, (s, p))
    fr_ref[t] = fs_ref[t]
    drain(fr_ref.at[pl.ds(0, NTGT - 1)], f_recv)
    out_ref[...] = jnp.sum(fr_ref[...], axis=0)

    drain(big_x.at[pl.ds(0, 7 * A_ROWS)], a_send)
    drain(big_x.at[pl.ds(0, 3 * B_ROWS)], b_send)
    drain(big_x.at[pl.ds(0, 24 * A_ROWS)], ya_send)
    drain(big_x.at[pl.ds(0, 28 * B_ROWS)], zb_send)
    drain(lk_ref.at[pl.ds(0, NTGT - 1)], lk_send)
    for sweep in range(SWEEPS):
        drain(rx_ref.at[sweep, pl.ds(0, NTGT - 1)], r_send.at[sweep])
        drain(cx_ref.at[sweep, pl.ds(0, NSRC - 1)], c_send.at[sweep])
    drain(fs_ref.at[pl.ds(0, NTGT - 1)], f_send)


def shards(
    source_embed,
    source_links,
    source_degree,
    target_embed,
    target_links,
    target_degree,
    w_self,
    w_neigh,
    cand_blocks,
    probe_pairs,
):
    slots = jnp.arange(KMAX, dtype=jnp.int32)[None, :]
    sl = jnp.where(slots < source_degree[:, None], source_links, -1).T
    sl = jnp.concatenate([sl, sl], axis=1)
    tl = jnp.where(slots < target_degree[:, None], target_links, -1).T
    pp = probe_pairs.reshape(R_BLK, BLK, QRY).transpose(0, 2, 1)

    local = cand_blocks - lax.axis_index("tgt") * C_LOC
    ids = jnp.arange(C_LOC, dtype=jnp.int32)
    match = local[:, :, None] == ids[None, None, :]
    hits = jnp.any(match, axis=1)
    blocks = jnp.arange(R_BLK, dtype=jnp.int32)
    earlier = blocks[None, :] < blocks[:, None]
    before = jnp.sum((earlier[:, :, None] & hits[None, :, :]).astype(jnp.int32), axis=1)
    place = jnp.where(hits, ids[None, :] * MOST + before, SLOTS)
    slot_ids = jnp.arange(SLOTS, dtype=jnp.int32)
    srow = jnp.sum(
        jnp.where(place.reshape(R_BLK, C_LOC, 1) == slot_ids[None, None, :], blocks[:, None, None] + 1, 0),
        axis=(0, 1),
    ) - 1
    tab = jnp.sum(jnp.where(match, place[:, None, :] + 1, 0), axis=2) - 1
    tab = jnp.pad(tab, ((0, 0), (0, BLK - CAND)), constant_values=-1).reshape(R_BLK, 1, BLK)

    vmem = pl.BlockSpec(memory_space=pltpu.VMEM)
    smem = pl.BlockSpec(memory_space=pltpu.SMEM)
    dma = pltpu.SemaphoreType.DMA
    packed = pl.pallas_call(
        sinkhorn_kernel,
        out_shape=jax.ShapeDtypeStruct((8, BLK), F32),
        in_specs=[smem, smem] + [vmem] * 8,
        out_specs=vmem,
        scratch_shapes=[
            pltpu.VMEM((WIDE // 16, 16, BLK), BF),
            pltpu.VMEM((NTGT * ROWS, D), BF),
            pltpu.VMEM((8, D, WIDE), BF),
            pltpu.VMEM((NTGT, KMAX, BLK), jnp.int32),
            pltpu.VMEM((8, NTGT * ROWS, WIDE), BF),
            pltpu.VMEM((R_BLK, D, BLK), BF),
            pltpu.VMEM((D, C_LOC * BLK), BF),
            pltpu.VMEM((C_LOC * BLK, WIDE), BF),
            pltpu.VMEM((C_LOC, BLK, D), BF),
            pltpu.VMEM((SLOTS, BLK, BLK), F32),
            pltpu.VMEM((SLOTS, BLK, BLK), F32),
            pltpu.VMEM((C_LOC, BLK, BLK), F32),
            pltpu.VMEM((SWEEPS, NTGT, R_BLK, BLK), F32),
            pltpu.VMEM((SWEEPS, NSRC, C_LOC, BLK), F32),
            pltpu.VMEM((R_BLK, BLK), F32),
            pltpu.VMEM((R_BLK, BLK), F32),
            pltpu.VMEM((R_BLK, BLK), F32),
            pltpu.VMEM((R_BLK, QRY, BLK), jnp.int32),
            pltpu.VMEM((SLOTS + 1, QRY, BLK), F32),
            pltpu.VMEM((R_BLK, QRY, BLK), F32),
            pltpu.VMEM((NTGT, 8, BLK), F32),
            pltpu.VMEM((NTGT, 8, BLK), F32),
            dma, dma((NZ,)), dma, dma((NY,)), dma, dma, dma, dma, dma, dma,
            dma((SWEEPS,)), dma((SWEEPS,)), dma((SWEEPS,)), dma((SWEEPS,)), dma, dma,
        ],
        compiler_params=pltpu.CompilerParams(
            collective_id=0, has_side_effects=True, vmem_limit_bytes=48 * 2**20
        ),
    )(
        srow, place.reshape(-1), source_embed, sl, target_embed, tl, w_self, w_neigh, tab, pp
    )
    return packed.reshape(8, 2, ROWS).transpose(2, 1, 0).reshape(ROWS, QRY)


def solution(mesh):
    placed = (
        P(("src", "tgt"), None),
        P(("src", "tgt"), None),
        P(("src", "tgt")),
        P("tgt", None),
        P("tgt", None),
        P("tgt"),
        P(),
        P(),
        P("src", None),
        P("src", None),
    )
    return jax.shard_map(
        shards, mesh=mesh, in_specs=placed, out_specs=P(("src", "tgt"), None), check_vma=False
    )
```

```python
import functools
import math

import jax
import jax.numpy as jnp
from jax import lax
from jax.experimental import pallas as pl
from jax.experimental.pallas import tpu as pltpu
from jax.sharding import PartitionSpec as P

D = 256
BLK = 128
CAND = 32
MOST = 4
QRY = 16
SWEEPS = 4
KMAX = 8
NY, NZ = 4, 8
NSRC, NTGT = 8, 32
ROWS = 64
R_BLK = 16
C_LOC = 8
SLOTS = C_LOC * MOST
A_ROWS = 48
B_ROWS = 16
WIDE = 256
NEG = -1e30
FLOOR = -1e29
SCALE = 3.0 / math.sqrt(D)
MESH = pl.DeviceIdType.MESH
BF = jnp.bfloat16
F32 = jnp.float32


def far_first():
    offs = [(dy, dz) for dy in range(NY) for dz in range(NZ) if (dy, dz) != (0, 0)]
    dist = lambda o: min(o[0], NY - o[0]) + min(o[1], NZ - o[1])
    return sorted(offs, key=lambda o: (-dist(o), o))


Z_FAR = (4, 3, 5, 2, 6, 1, 7)
Z_NEAR = (1, 7, 2, 6, 3, 5, 4)
Y_FAR = (2, 1, 3)


def sinkhorn_kernel(
    x_hbm, sl_hbm, sd_hbm, t_hbm, tl_hbm, td_hbm, ws_hbm, wn_hbm, cand_hbm, pp_hbm,
    out_ref,
    sl_ref, sd_ref, t_ref, tl_ref, td_ref, ws_ref, wn_ref, cand_ref, pq_ref,
    tab_ref, pp_ref, meta_ref, meta_s, acc_ref, in_sem, meta_sem,
    iota_ref, big_x, xt_ref, lk_ref, at_ref, ht_ref, tt_ref, att_ref, th_ref,
    s_ref, e_ref, wb_ref, rx_ref, rh_ref, cx_ref, top_ref, r0_ref, u_ref, sid_ref, g_ref, pk_ref,
    fs_ref, fr_ref,
    a_send, a_recv, b_send, b_recv, ya_send, ya_recv, zb_send, zb_recv, lk_send, lk_recv,
    r_send, r_recv, c_send, c_recv, f_send, f_recv,
):
    s = lax.axis_index("src")
    t = lax.axis_index("tgt")
    y = t // NZ
    z = lax.rem(t, NZ)
    tgt_peers = [lax.rem(y + dy, NY) * NZ + lax.rem(z + dz, NZ) for dy, dz in far_first()]
    sx = s // 2
    score = lax.rem(s, 2)
    src_peers = [
        lax.rem(sx + dx, 4) * 2 + (score if same else 1 - score)
        for dx, same in ((2, False), (2, True), (1, False), (3, False), (1, True), (3, True), (0, False))
    ]

    staged = (
        (sl_hbm, sl_ref), (sd_hbm, sd_ref), (cand_hbm, cand_ref), (tl_hbm, tl_ref), (td_hbm, td_ref),
        (t_hbm, t_ref), (ws_hbm, ws_ref), (wn_hbm, wn_ref), (pp_hbm, pq_ref),
        (x_hbm, big_x.at[pl.ds(t * ROWS, ROWS)]),
    )
    loads = [pltpu.make_async_copy(src, dst, in_sem.at[i]) for i, (src, dst) in enumerate(staged)]
    for load in loads:
        load.start()

    barrier = pltpu.get_barrier_semaphore()
    for p in tgt_peers:
        pl.semaphore_signal(barrier, inc=1, device_id=(s, p), device_id_type=MESH)
    for p in src_peers:
        pl.semaphore_signal(barrier, inc=1, device_id=(p, t), device_id_type=MESH)

    tile_rows = lax.broadcasted_iota(jnp.int32, (WIDE // 16, 16, BLK), 0) * 16
    tile_rows = tile_rows + lax.broadcasted_iota(jnp.int32, (WIDE // 16, 16, BLK), 1)
    iota_ref[...] = tile_rows.astype(jnp.int16)
    lane4 = lax.broadcasted_iota(jnp.int32, (KMAX // 2, BLK), 1)
    loads[0].wait()
    loads[1].wait()
    slot8 = lax.broadcasted_iota(jnp.int32, (KMAX, ROWS), 0)
    own = jnp.where(slot8 < sd_ref[...], sl_ref[...], -1)
    own = jnp.concatenate([own, own], axis=1)
    lk_ref[t] = jnp.where(lane4 < ROWS, own[:4], own[4:])

    loads[2].wait()
    local = cand_ref[...] - t * C_LOC
    local = jnp.concatenate([local, jnp.full((R_BLK, BLK - CAND), -1, jnp.int32)], axis=1)
    lane16 = lax.broadcasted_iota(jnp.int32, (R_BLK, BLK), 1)
    row16 = lax.broadcasted_iota(jnp.int32, (R_BLK, BLK), 0)
    hits = jnp.zeros((R_BLK, BLK), jnp.int32)
    for c in range(C_LOC):
        named = jnp.max(jnp.where(local == c, 1, 0), axis=1, keepdims=True)
        hits = jnp.where(lane16 == c, named, hits)
    before = jnp.zeros((R_BLK, BLK), jnp.int32)
    for r in range(R_BLK - 1):
        before = before + jnp.where(row16 > r, hits[r : r + 1, :], 0)
    place = jnp.where(hits > 0, lane16 * MOST + before, SLOTS)
    meta_ref[:R_BLK, :] = place
    rows_of_slot = [
        jnp.sum(
            jnp.where((hits > 0) & (before == m), row16 + 1, 0), axis=0, keepdims=True
        )
        for m in range(MOST)
    ]
    pad4 = jnp.zeros((8 - MOST, BLK), jnp.int32)
    meta_ref[R_BLK:, :] = jnp.concatenate(rows_of_slot + [pad4], axis=0) - 1
    table = jnp.full((R_BLK, BLK), -1, jnp.int32)
    for c in range(C_LOC):
        table = jnp.where(local == c, jnp.broadcast_to(place[:, c : c + 1], (R_BLK, BLK)), table)
    tab_ref[...] = table
    to_scalar = pltpu.make_async_copy(meta_ref, meta_s, meta_sem)
    to_scalar.start()

    def row_of(c, m):
        return meta_s[R_BLK + m, c]

    def row_at(c, m):
        return jnp.clip(row_of(c, m), 0, R_BLK - 1)

    g_ref[SLOTS] = jnp.zeros((QRY, BLK), F32)

    for load in loads[3:]:
        load.wait()
    for block in range(R_BLK):
        pp_ref[block] = pq_ref[:, block * BLK : (block + 1) * BLK]
    ws_t = ws_ref[...].T
    wn_t = wn_ref[...].T
    for chunk in range(4):
        tt_ref[:, chunk * WIDE : (chunk + 1) * WIDE] = t_ref[chunk * WIDE : (chunk + 1) * WIDE, :].T

    def build(links, chunks, put):
        singles = [part[k : k + 1, :] for part in links for k in range(part.shape[0])]
        rows, counts = [], []
        for part in links:
            count = jnp.zeros(part.shape, F32)
            for single in singles:
                count = count + jnp.where(part == single, 1.0, 0.0)
            counts += [
                jnp.broadcast_to(count[k : k + 1, :], (16, BLK)).astype(BF) for k in range(part.shape[0])
            ]
        for single in singles:
            rows.append(jnp.broadcast_to(single, (16, BLK)).astype(jnp.int16))

        def body(q, _):
            base = jnp.full((16, BLK), q * WIDE, jnp.int32).astype(jnp.int16)
            total = jnp.zeros((WIDE // 16, 16, BLK), BF)
            for k in range(KMAX):
                total = jnp.where((rows[k] - base)[None] == iota_ref[...], counts[k][None], total)
            put(q, total.reshape(WIDE, BLK))
            return 0

        lax.fori_loop(0, chunks, body, 0)

    def encode(table_t, adjacency, own_t, degree):
        total = jnp.dot(table_t, adjacency, preferred_element_type=F32)
        mean = (total / degree).astype(BF)
        mixed = jnp.dot(ws_t, own_t, preferred_element_type=F32) + jnp.dot(
            wn_t, mean, preferred_element_type=F32
        )
        return mixed.astype(BF)

    for chunk in range(4):
        cols = slice(chunk * WIDE, (chunk + 1) * WIDE)
        degree = td_ref[:, cols]
        slot_rows = lax.broadcasted_iota(jnp.int32, (KMAX, WIDE), 0)
        links = jnp.where(slot_rows < degree, tl_ref[:, cols], -1)
        degree = degree.astype(F32)
        for half in range(2):
            def put(q, value, half=half):
                att_ref[pl.ds(q * WIDE, WIDE), half * BLK : (half + 1) * BLK] = value

            build([links[:, half * BLK : (half + 1) * BLK]], 4, put)
        coded = encode(tt_ref[...], att_ref[...], tt_ref[:, cols], degree).T
        th_ref[2 * chunk] = coded[:BLK]
        th_ref[2 * chunk + 1] = coded[BLK:]

    pl.semaphore_wait(barrier, NTGT - 1 + NSRC - 1)

    def push(src, dst, ssem, rsem, dev):
        pltpu.make_async_remote_copy(
            src_ref=src, dst_ref=dst, send_sem=ssem, recv_sem=rsem, device_id=dev, device_id_type=MESH
        ).start()

    def drain(ref, sem):
        pltpu.make_async_copy(ref, ref, sem).wait()

    def part_a(d):
        return big_x.at[pl.ds(d * ROWS, A_ROWS)]

    def part_b(d):
        return big_x.at[pl.ds(d * ROWS + A_ROWS, B_ROWS)]

    def at_yz(dy, dz):
        return lax.rem(y + dy + NY, NY) * NZ + lax.rem(z + dz + NZ, NZ)

    for k in Z_FAR:
        push(part_a(t), part_a(t), a_send, a_recv.at[k], (s, at_yz(0, k)))
    for j in Y_FAR:
        push(part_b(t), part_b(t), b_send, b_recv.at[j], (s, at_yz(j, 0)))
    for p in tgt_peers:
        push(lk_ref.at[t], lk_ref.at[t], lk_send, lk_recv, (s, p))
    for j in Y_FAR:
        push(part_a(t), part_a(t), ya_send, ya_recv.at[j], (s, at_yz(j, 0)))
    for k in Z_FAR:
        push(part_b(t), part_b(t), zb_send, zb_recv.at[0], (s, at_yz(0, k)))

    for j in Y_FAR[::-1]:
        drain(part_b(t), b_recv.at[j])
        d = at_yz(-j, 0)
        for k in Z_FAR:
            push(part_b(d), part_b(d), zb_send, zb_recv.at[j], (s, at_yz(0, k)))
    for k in Z_NEAR:
        drain(part_a(t), a_recv.at[k])
        d = at_yz(0, -k)
        for j in Y_FAR:
            push(part_a(d), part_a(d), ya_send, ya_recv.at[j], (s, at_yz(j, 0)))

    drain(lk_ref.at[pl.ds(0, NTGT - 1)], lk_recv)

    def group_links(block):
        first, second = lk_ref[2 * block], lk_ref[2 * block + 1]
        return [
            jnp.where(lane4 < ROWS, first, pltpu.roll(second, ROWS, 1)),
            jnp.where(lane4 < ROWS, pltpu.roll(first, ROWS, 1), second),
        ]

    def build_pair(pair, _):
        for half in range(2):
            def put(q, value, half=half):
                at_ref[pair, pl.ds(q * WIDE, WIDE), half * BLK : (half + 1) * BLK] = value

            build(group_links(2 * pair + half), 8, put)
        return 0

    lax.fori_loop(0, 8, build_pair, 0)

    for step, j in enumerate((0, 1, 3, 2)):
        if j:
            drain(big_x.at[pl.ds(0, NZ * A_ROWS)], ya_recv.at[j])
        drain(big_x.at[pl.ds(0, (NZ - 1) * B_ROWS)], zb_recv.at[j])
        pair_base = lax.rem(y - j + NY, NY) * 2
        for h in range(2):
            q = pair_base + h
            xt_ref[q] = big_x[pl.ds(pl.multiple_of(q * WIDE, WIDE), WIDE), :].T

        def add_pair(pair, _):
            total = None if step == 0 else acc_ref[pair]
            for h in range(2):
                q = pair_base + h
                part = jnp.dot(
                    xt_ref[q], at_ref[pair, pl.ds(pl.multiple_of(q * WIDE, WIDE), WIDE), :],
                    preferred_element_type=F32,
                )
                total = part if total is None else total + part
            if step < NY - 1:
                acc_ref[pair] = total
                return 0
            links = [
                jnp.concatenate(parts, axis=1)
                for parts in zip(group_links(2 * pair), group_links(2 * pair + 1))
            ]
            degree = sum(jnp.sum((part >= 0).astype(F32), axis=0, keepdims=True) for part in links)
            mean = (total / degree).astype(BF)
            mixed = jnp.dot(ws_t, xt_ref[pair], preferred_element_type=F32) + jnp.dot(
                wn_t, mean, preferred_element_type=F32
            )
            coded = mixed.astype(BF)
            ht_ref[2 * pair] = coded[:, :BLK]
            ht_ref[2 * pair + 1] = coded[:, BLK:]
            return 0

        lax.fori_loop(0, 8, add_pair, 0)

    to_scalar.wait()
    block_id = lax.broadcasted_iota(jnp.int32, (R_BLK, BLK), 0)
    lane = lax.broadcasted_iota(jnp.int32, (BLK, BLK), 1)
    neg16 = jnp.full((R_BLK, BLK), NEG, F32)

    def score_block(c, best):
        for m in range(MOST):
            r = row_of(c, m)
            bias = jnp.where(r < 0, NEG, 0.0)
            raw = jnp.dot(th_ref[c], ht_ref[row_at(c, m)], preferred_element_type=F32)
            raw = raw * SCALE + bias
            s_ref[c * MOST + m] = raw
            best = jnp.maximum(best, jnp.where(block_id == r, jnp.max(raw, axis=0, keepdims=True), NEG))
        return best

    top = lax.fori_loop(0, C_LOC, score_block, neg16)
    top_ref[...] = top

    def first_rows(c, total):
        for m in range(MOST):
            r = row_of(c, m)
            high = top_ref[pl.ds(row_at(c, m), 1), :]
            part = jnp.sum(jnp.exp(s_ref[c * MOST + m] - high), axis=0, keepdims=True)
            total = total + jnp.where(block_id == r, part, 0.0)
        return total

    total = lax.fori_loop(0, C_LOC, first_rows, jnp.zeros((R_BLK, BLK), F32))
    rx_ref[0, t] = jnp.where(total > 0.0, top + jnp.log(total), NEG)

    def send_rows(sweep, buf, slot):
        for p in tgt_peers:
            push(buf.at[slot, t], buf.at[slot, t], r_send.at[sweep], r_recv.at[sweep], (s, p))

    def await_rows(sweep, buf, slot):
        drain(buf.at[slot, pl.ds(0, NTGT - 1)], r_recv.at[sweep])
        return buf[slot]

    def send_cols(sweep):
        for p in src_peers:
            push(cx_ref.at[sweep, s], cx_ref.at[sweep, s], c_send.at[sweep], c_recv.at[sweep], (p, t))

    def await_cols(sweep):
        drain(cx_ref.at[sweep, pl.ds(0, NSRC - 1)], c_recv.at[sweep])
        return cx_ref[sweep]

    send_rows(0, rx_ref, 0)

    def probe_slots(block, _):
        table = jnp.broadcast_to(tab_ref[pl.ds(block, 1), :], (8, BLK))
        for half in range(2):
            rows = slice(half * 8, half * 8 + 8)
            which = pp_ref[block, rows, :] // BLK
            sid_ref[block, rows, :] = jnp.take_along_axis(table, which, axis=1)
        return 0

    lax.fori_loop(0, R_BLK, probe_slots, 0)

    def pick(slot, _):
        r = row_at(slot // MOST, lax.rem(slot, MOST))
        for half in range(2):
            rows = slice(half * 8, half * 8 + 8)
            offset = lax.rem(pp_ref[r, rows, :], BLK)
            strip, inner = offset // 8, lax.rem(offset, 8)
            value = jnp.zeros((8, BLK), F32)
            for k in range(BLK // 8):
                got = jnp.take_along_axis(s_ref[slot, k * 8 : k * 8 + 8, :], inner, axis=0)
                value = jnp.where(strip == k, got, value)
            g_ref[slot, rows, :] = jnp.where(sid_ref[r, rows, :] == slot, value, 0.0)
        return 0

    lax.fori_loop(0, SLOTS, pick, 0)

    def merge(block, _):
        total = jnp.zeros((QRY, BLK), F32)
        for c in range(C_LOC):
            total = total + g_ref[jnp.clip(meta_s[block, c], 0, SLOTS)]
        pk_ref[block] = total
        return 0

    lax.fori_loop(0, R_BLK, merge, 0)

    parts = await_rows(0, rx_ref, 0)
    high = jnp.max(parts, axis=0)
    r0 = -(high + jnp.log(jnp.sum(jnp.exp(parts - high[None]), axis=0)))
    r0_ref[...] = r0

    def first_cols(c, carry):
        tops, sums = carry
        shifted = [
            s_ref[c * MOST + m] + r0_ref[pl.ds(row_at(c, m), 1), :]
            for m in range(MOST)
        ]
        high = functools.reduce(jnp.maximum, shifted)
        high = jnp.maximum(jnp.max(high, axis=1, keepdims=True), FLOOR)
        total = jnp.zeros((BLK, BLK), F32)
        for m in range(MOST):
            e = jnp.exp(shifted[m] - high)
            e_ref[c * MOST + m] = e
            total = total + e
        total = jnp.sum(total, axis=1, keepdims=True)
        return jnp.where(lane == c, high, tops), jnp.where(lane == c, total, sums)

    zero_tile = jnp.zeros((BLK, BLK), F32)
    tops, sums = lax.fori_loop(0, C_LOC, first_cols, (zero_tile, zero_tile))
    tops = tops.T[:C_LOC]
    sums = sums.T[:C_LOC]
    cx_ref[0, s] = jnp.where(sums > 0.0, tops + jnp.log(sums), NEG)
    send_cols(0)
    parts = await_cols(0)
    high = jnp.max(parts, axis=0)
    share = R_BLK * BLK * NSRC / (C_LOC * BLK * NTGT)
    c0 = math.log(share) - (high + jnp.log(jnp.sum(jnp.exp(parts - high[None]), axis=0)))
    factor = jnp.exp(tops + c0)

    def spread(weights):
        upright = jnp.concatenate([weights, jnp.zeros((BLK - C_LOC, BLK), F32)], axis=0).T
        for c in range(C_LOC):
            wb_ref[c] = jnp.broadcast_to(upright[:, c : c + 1], (BLK, BLK))

    def sweep_body(sweep, carry, rows_buf):
        _, col_scale = carry
        spread(factor * col_scale)

        def rows_of(c, total):
            for m in range(MOST):
                part = jnp.sum(e_ref[c * MOST + m] * wb_ref[c], axis=0, keepdims=True)
                total = total + jnp.where(block_id == row_of(c, m), part, 0.0)
            return total

        total = lax.fori_loop(0, C_LOC, rows_of, jnp.zeros((R_BLK, BLK), F32))
        slot = 1 if rows_buf is rx_ref else sweep - 1
        rows_buf[slot, t] = total.astype(rows_buf.dtype)
        send_rows(sweep, rows_buf, slot)
        parts = await_rows(sweep, rows_buf, slot)
        row_scale = 1.0 / jnp.sum(parts.astype(F32), axis=0)
        u_ref[...] = row_scale

        def cols_of(c, sums):
            total = jnp.zeros((BLK, BLK), F32)
            for m in range(MOST):
                r = row_at(c, m)
                total = total + e_ref[c * MOST + m] * u_ref[pl.ds(r, 1), :]
            return jnp.where(lane == c, jnp.sum(total, axis=1, keepdims=True), sums)

        sums = lax.fori_loop(0, C_LOC, cols_of, zero_tile).T[:C_LOC]
        cx_ref[sweep, s] = sums * factor
        send_cols(sweep)
        return row_scale, share / jnp.sum(await_cols(sweep), axis=0)

    scales = (jnp.ones((R_BLK, BLK), F32), jnp.ones((C_LOC, BLK), F32))
    scales = lax.fori_loop(1, SWEEPS - 1, lambda i, carry: sweep_body(i, carry, rh_ref), scales)
    row_scale, col_scale = sweep_body(SWEEPS - 1, scales, rx_ref)
    row_pot = r0 + jnp.log(row_scale)
    col_pot = c0 + jnp.log(col_scale) + math.log(CAND * BLK)
    u_ref[...] = row_pot
    top_ref[:C_LOC, :] = col_pot
    lane8 = lax.broadcasted_iota(jnp.int32, (8, BLK), 1)

    def finish(block, _):
        done = []
        for half in range(2):
            rows = slice(half * 8, half * 8 + 8)
            sid = sid_ref[block, rows, :]
            offset = lax.rem(pp_ref[block, rows, :], BLK)
            owner = sid // MOST
            value = jnp.zeros((8, BLK), F32)
            for c in range(C_LOC):
                strip = jnp.broadcast_to(top_ref[c : c + 1, :], (8, BLK))
                value = jnp.where(owner == c, jnp.take_along_axis(strip, offset, axis=1), value)
            value = value + pk_ref[block, rows, :] + u_ref[pl.ds(block, 1), :]
            done.append(jnp.where(sid >= 0, value, 0.0))
        low, high = done
        fs_ref[2 * block] = jnp.where(lane8 < ROWS, low, pltpu.roll(high, ROWS, 1))
        fs_ref[2 * block + 1] = jnp.where(lane8 < ROWS, pltpu.roll(low, ROWS, 1), high)
        return 0

    lax.fori_loop(0, R_BLK, finish, 0)
    for p in tgt_peers:
        push(fs_ref.at[p], fr_ref.at[t], f_send, f_recv, (s, p))
    fr_ref[t] = fs_ref[t]
    drain(fr_ref.at[pl.ds(0, NTGT - 1)], f_recv)
    out_ref[...] = jnp.sum(fr_ref[...], axis=0)

    drain(big_x.at[pl.ds(0, 7 * A_ROWS)], a_send)
    drain(big_x.at[pl.ds(0, 3 * B_ROWS)], b_send)
    drain(big_x.at[pl.ds(0, 24 * A_ROWS)], ya_send)
    drain(big_x.at[pl.ds(0, 28 * B_ROWS)], zb_send)
    drain(lk_ref.at[pl.ds(0, NTGT - 1)], lk_send)
    for sweep in range(SWEEPS):
        rows_sent = rh_ref.at[sweep - 1] if 0 < sweep < SWEEPS - 1 else rx_ref.at[min(sweep, 1)]
        drain(rows_sent.at[pl.ds(0, NTGT - 1)], r_send.at[sweep])
        drain(cx_ref.at[sweep, pl.ds(0, NSRC - 1)], c_send.at[sweep])
    drain(fs_ref.at[pl.ds(0, NTGT - 1)], f_send)


def shards(
    source_embed,
    source_links,
    source_degree,
    target_embed,
    target_links,
    target_degree,
    w_self,
    w_neigh,
    cand_blocks,
    probe_pairs,
):
    vmem = pl.BlockSpec(memory_space=pltpu.VMEM)
    hbm = pl.BlockSpec(memory_space=pltpu.HBM)
    dma = pltpu.SemaphoreType.DMA
    packed = pl.pallas_call(
        sinkhorn_kernel,
        out_shape=jax.ShapeDtypeStruct((8, BLK), F32),
        in_specs=[hbm] * 10,
        out_specs=vmem,
        scratch_shapes=[
            pltpu.VMEM((KMAX, ROWS), jnp.int32),
            pltpu.VMEM((1, ROWS), jnp.int32),
            pltpu.VMEM((C_LOC * BLK, D), BF),
            pltpu.VMEM((KMAX, C_LOC * BLK), jnp.int32),
            pltpu.VMEM((1, C_LOC * BLK), jnp.int32),
            pltpu.VMEM((D, D), BF),
            pltpu.VMEM((D, D), BF),
            pltpu.VMEM((R_BLK, CAND), jnp.int32),
            pltpu.VMEM((QRY, R_BLK * BLK), jnp.int32),
            pltpu.VMEM((R_BLK, BLK), jnp.int32),
            pltpu.VMEM((R_BLK, QRY, BLK), jnp.int32),
            pltpu.VMEM((R_BLK + 8, BLK), jnp.int32),
            pltpu.SMEM((R_BLK + 8, BLK), jnp.int32),
            pltpu.VMEM((8, D, WIDE), F32),
            dma((10,)),
            dma,
            pltpu.VMEM((WIDE // 16, 16, BLK), jnp.int16),
            pltpu.VMEM((NTGT * ROWS, D), BF),
            pltpu.VMEM((8, D, WIDE), BF),
            pltpu.VMEM((NTGT, KMAX // 2, BLK), jnp.int32),
            pltpu.VMEM((8, NTGT * ROWS, WIDE), BF),
            pltpu.VMEM((R_BLK, D, BLK), BF),
            pltpu.VMEM((D, C_LOC * BLK), BF),
            pltpu.VMEM((C_LOC * BLK, WIDE), BF),
            pltpu.VMEM((C_LOC, BLK, D), BF),
            pltpu.VMEM((SLOTS, BLK, BLK), F32),
            pltpu.VMEM((SLOTS, BLK, BLK), F32),
            pltpu.VMEM((C_LOC, BLK, BLK), F32),
            pltpu.VMEM((2, NTGT, R_BLK, BLK), F32),
            pltpu.VMEM((SWEEPS - 2, NTGT, R_BLK, BLK), BF),
            pltpu.VMEM((SWEEPS, NSRC, C_LOC, BLK), F32),
            pltpu.VMEM((R_BLK, BLK), F32),
            pltpu.VMEM((R_BLK, BLK), F32),
            pltpu.VMEM((R_BLK, BLK), F32),
            pltpu.VMEM((R_BLK, QRY, BLK), jnp.int32),
            pltpu.VMEM((SLOTS + 1, QRY, BLK), F32),
            pltpu.VMEM((R_BLK, QRY, BLK), F32),
            pltpu.VMEM((NTGT, 8, BLK), F32),
            pltpu.VMEM((NTGT, 8, BLK), F32),
            dma, dma((NZ,)), dma, dma((NY,)), dma, dma((NY,)), dma, dma((NY,)), dma, dma,
            dma((SWEEPS,)), dma((SWEEPS,)), dma((SWEEPS,)), dma((SWEEPS,)), dma, dma,
        ],
        compiler_params=pltpu.CompilerParams(
            collective_id=0, has_side_effects=True, vmem_limit_bytes=64 * 2**20
        ),
    )(
        source_embed, source_links.T, source_degree.reshape(1, -1), target_embed, target_links.T,
        target_degree.reshape(1, -1), w_self, w_neigh, cand_blocks, probe_pairs.T,
    )
    return packed.reshape(8, 2, ROWS).transpose(2, 1, 0).reshape(ROWS, QRY)


def solution(mesh):
    placed = (
        P(("src", "tgt"), None),
        P(("src", "tgt"), None),
        P(("src", "tgt")),
        P("tgt", None),
        P("tgt", None),
        P("tgt"),
        P(),
        P(),
        P("src", None),
        P("src", None),
    )
    return jax.shard_map(
        shards, mesh=mesh, in_specs=placed, out_specs=P(("src", "tgt"), None), check_vma=False
    )
```

```python
import functools
import math

import jax
import jax.numpy as jnp
from jax import lax
from jax.experimental import pallas as pl
from jax.experimental.pallas import tpu as pltpu
from jax.sharding import PartitionSpec as P

D = 256
BLK = 128
CAND = 32
MOST = 4
QRY = 16
SWEEPS = 4
KMAX = 8
NY, NZ = 4, 8
NSRC, NTGT = 8, 32
ROWS = 64
R_BLK = 16
C_LOC = 8
SLOTS = C_LOC * MOST
A_ROWS = 48
B_ROWS = 16
WIDE = 256
NEG = -1e30
FLOOR = -1e29
SCALE = 3.0 / math.sqrt(D)
MESH = pl.DeviceIdType.MESH
BF = jnp.bfloat16
F32 = jnp.float32


def far_first():
    offs = [(dy, dz) for dy in range(NY) for dz in range(NZ) if (dy, dz) != (0, 0)]
    dist = lambda o: min(o[0], NY - o[0]) + min(o[1], NZ - o[1])
    return sorted(offs, key=lambda o: (-dist(o), o))


Z_FAR = (4, 3, 5, 2, 6, 1, 7)
Z_NEAR = (1, 7, 2, 6, 3, 5, 4)
Y_FAR = (2, 1, 3)


def sinkhorn_kernel(
    x_hbm, sl_hbm, sd_hbm, t_hbm, tl_hbm, td_hbm, ws_hbm, wn_hbm, cand_hbm, pp_hbm,
    out_ref,
    sl_ref, sd_ref, t_ref, tl_ref, td_ref, ws_ref, wn_ref, cand_ref, pq_ref,
    tab_ref, pp_ref, meta_ref, meta_s, acc_ref, in_sem, meta_sem,
    iota_ref, big_x, xt_ref, lk_ref, at_ref, ht_ref, tt_ref, att_ref, th_ref,
    s_ref, e_ref, wb_ref, rx_ref, rh_ref, cx_ref, top_ref, r0_ref, u_ref, sid_ref, g_ref, pk_ref,
    fs_ref, fr_ref,
    a_send, a_recv, b_send, b_recv, ya_send, ya_recv, zb_send, zb_recv, lk_send, lk_recv,
    r_send, r_recv, c_send, c_recv, f_send, f_recv,
):
    s = lax.axis_index("src")
    t = lax.axis_index("tgt")
    y = t // NZ
    z = lax.rem(t, NZ)
    tgt_peers = [lax.rem(y + dy, NY) * NZ + lax.rem(z + dz, NZ) for dy, dz in far_first()]
    sx = s // 2
    score = lax.rem(s, 2)
    src_peers = [
        lax.rem(sx + dx, 4) * 2 + (score if same else 1 - score)
        for dx, same in ((2, False), (2, True), (1, False), (3, False), (1, True), (3, True), (0, False))
    ]

    staged = (
        (sl_hbm, sl_ref), (sd_hbm, sd_ref), (cand_hbm, cand_ref), (tl_hbm, tl_ref), (td_hbm, td_ref),
        (t_hbm, t_ref), (ws_hbm, ws_ref), (wn_hbm, wn_ref), (pp_hbm, pq_ref),
        (x_hbm, big_x.at[pl.ds(t * ROWS, ROWS)]),
    )
    loads = [pltpu.make_async_copy(src, dst, in_sem.at[i]) for i, (src, dst) in enumerate(staged)]
    for load in loads:
        load.start()

    barrier = pltpu.get_barrier_semaphore()
    for p in tgt_peers:
        pl.semaphore_signal(barrier, inc=1, device_id=(s, p), device_id_type=MESH)
    for p in src_peers:
        pl.semaphore_signal(barrier, inc=1, device_id=(p, t), device_id_type=MESH)

    tile_rows = lax.broadcasted_iota(jnp.int32, (WIDE // 16, 16, BLK), 0) * 16
    tile_rows = tile_rows + lax.broadcasted_iota(jnp.int32, (WIDE // 16, 16, BLK), 1)
    iota_ref[...] = tile_rows.astype(jnp.int16)
    lane4 = lax.broadcasted_iota(jnp.int32, (KMAX // 2, BLK), 1)
    loads[0].wait()
    loads[1].wait()
    slot8 = lax.broadcasted_iota(jnp.int32, (KMAX, ROWS), 0)
    own = jnp.where(slot8 < sd_ref[...], sl_ref[...], -1)
    own = jnp.concatenate([own, own], axis=1)
    lk_ref[t] = jnp.where(lane4 < ROWS, own[:4], own[4:])

    loads[2].wait()
    local = cand_ref[...] - t * C_LOC
    local = jnp.concatenate([local, jnp.full((R_BLK, BLK - CAND), -1, jnp.int32)], axis=1)
    lane16 = lax.broadcasted_iota(jnp.int32, (R_BLK, BLK), 1)
    row16 = lax.broadcasted_iota(jnp.int32, (R_BLK, BLK), 0)
    hits = jnp.zeros((R_BLK, BLK), jnp.int32)
    for c in range(C_LOC):
        named = jnp.max(jnp.where(local == c, 1, 0), axis=1, keepdims=True)
        hits = jnp.where(lane16 == c, named, hits)
    before = jnp.zeros((R_BLK, BLK), jnp.int32)
    for r in range(R_BLK - 1):
        before = before + jnp.where(row16 > r, hits[r : r + 1, :], 0)
    place = jnp.where(hits > 0, lane16 * MOST + before, SLOTS)
    meta_ref[:R_BLK, :] = place
    rows_of_slot = [
        jnp.sum(
            jnp.where((hits > 0) & (before == m), row16 + 1, 0), axis=0, keepdims=True
        )
        for m in range(MOST)
    ]
    pad4 = jnp.zeros((8 - MOST, BLK), jnp.int32)
    meta_ref[R_BLK:, :] = jnp.concatenate(rows_of_slot + [pad4], axis=0) - 1
    table = jnp.full((R_BLK, BLK), -1, jnp.int32)
    for c in range(C_LOC):
        table = jnp.where(local == c, jnp.broadcast_to(place[:, c : c + 1], (R_BLK, BLK)), table)
    tab_ref[...] = table
    to_scalar = pltpu.make_async_copy(meta_ref, meta_s, meta_sem)
    to_scalar.start()

    def row_of(c, m):
        return meta_s[R_BLK + m, c]

    def row_at(c, m):
        return jnp.clip(row_of(c, m), 0, R_BLK - 1)

    g_ref[SLOTS] = jnp.zeros((QRY, BLK), F32)

    for load in loads[3:]:
        load.wait()
    for block in range(R_BLK):
        pp_ref[block] = pq_ref[:, block * BLK : (block + 1) * BLK]
    ws_t = ws_ref[...].T
    wn_t = wn_ref[...].T
    for chunk in range(4):
        tt_ref[:, chunk * WIDE : (chunk + 1) * WIDE] = t_ref[chunk * WIDE : (chunk + 1) * WIDE, :].T

    def build(links, chunks, put):
        singles = [part[k : k + 1, :] for part in links for k in range(part.shape[0])]
        rows, counts = [], []
        for part in links:
            count = jnp.zeros(part.shape, F32)
            for single in singles:
                count = count + jnp.where(part == single, 1.0, 0.0)
            counts += [
                jnp.broadcast_to(count[k : k + 1, :], (16, BLK)).astype(BF) for k in range(part.shape[0])
            ]
        for single in singles:
            rows.append(jnp.broadcast_to(single, (16, BLK)).astype(jnp.int16))

        def body(q, _):
            base = jnp.full((16, BLK), q * WIDE, jnp.int32).astype(jnp.int16)
            total = jnp.zeros((WIDE // 16, 16, BLK), BF)
            for k in range(KMAX):
                total = jnp.where((rows[k] - base)[None] == iota_ref[...], counts[k][None], total)
            put(q, total.reshape(WIDE, BLK))
            return 0

        lax.fori_loop(0, chunks, body, 0)

    def encode(table_t, adjacency, own_t, degree):
        total = jnp.dot(table_t, adjacency, preferred_element_type=F32)
        mean = (total / degree).astype(BF)
        mixed = jnp.dot(ws_t, own_t, preferred_element_type=F32) + jnp.dot(
            wn_t, mean, preferred_element_type=F32
        )
        return mixed.astype(BF)

    for chunk in range(4):
        cols = slice(chunk * WIDE, (chunk + 1) * WIDE)
        degree = td_ref[:, cols]
        slot_rows = lax.broadcasted_iota(jnp.int32, (KMAX, WIDE), 0)
        links = jnp.where(slot_rows < degree, tl_ref[:, cols], -1)
        degree = degree.astype(F32)
        for half in range(2):
            def put(q, value, half=half):
                att_ref[pl.ds(q * WIDE, WIDE), half * BLK : (half + 1) * BLK] = value

            build([links[:, half * BLK : (half + 1) * BLK]], 4, put)
        coded = encode(tt_ref[...], att_ref[...], tt_ref[:, cols], degree).T
        th_ref[2 * chunk] = coded[:BLK]
        th_ref[2 * chunk + 1] = coded[BLK:]

    pl.semaphore_wait(barrier, NTGT - 1 + NSRC - 1)

    def push(src, dst, ssem, rsem, dev):
        pltpu.make_async_remote_copy(
            src_ref=src, dst_ref=dst, send_sem=ssem, recv_sem=rsem, device_id=dev, device_id_type=MESH
        ).start()

    def drain(ref, sem):
        pltpu.make_async_copy(ref, ref, sem).wait()

    def part_a(d):
        return big_x.at[pl.ds(d * ROWS, A_ROWS)]

    def part_b(d):
        return big_x.at[pl.ds(d * ROWS + A_ROWS, B_ROWS)]

    def at_yz(dy, dz):
        return lax.rem(y + dy + NY, NY) * NZ + lax.rem(z + dz + NZ, NZ)

    for p in tgt_peers:
        push(lk_ref.at[t], lk_ref.at[t], lk_send, lk_recv, (s, p))
    for k in Z_FAR:
        push(part_a(t), part_a(t), a_send, a_recv.at[k], (s, at_yz(0, k)))
    for j in Y_FAR:
        push(part_b(t), part_b(t), b_send, b_recv.at[j], (s, at_yz(j, 0)))
    for j in Y_FAR:
        push(part_a(t), part_a(t), ya_send, ya_recv.at[j], (s, at_yz(j, 0)))
    for k in Z_FAR:
        push(part_b(t), part_b(t), zb_send, zb_recv.at[0], (s, at_yz(0, k)))

    for j in Y_FAR[::-1]:
        drain(part_b(t), b_recv.at[j])
        d = at_yz(-j, 0)
        for k in Z_FAR:
            push(part_b(d), part_b(d), zb_send, zb_recv.at[j], (s, at_yz(0, k)))
    def relay(near):
        for k in near:
            drain(part_a(t), a_recv.at[k])
            d = at_yz(0, -k)
            for j in Y_FAR:
                push(part_a(d), part_a(d), ya_send, ya_recv.at[j], (s, at_yz(j, 0)))

    relay(Z_NEAR[:4])
    drain(lk_ref.at[pl.ds(0, NTGT - 1)], lk_recv)

    def group_links(block):
        first, second = lk_ref[2 * block], lk_ref[2 * block + 1]
        return [
            jnp.where(lane4 < ROWS, first, pltpu.roll(second, ROWS, 1)),
            jnp.where(lane4 < ROWS, pltpu.roll(first, ROWS, 1), second),
        ]

    def build_pair(pair, _):
        for half in range(2):
            def put(q, value, half=half):
                at_ref[pair, pl.ds(q * WIDE, WIDE), half * BLK : (half + 1) * BLK] = value

            build(group_links(2 * pair + half), 8, put)
        return 0

    lax.fori_loop(0, 2, build_pair, 0)
    relay(Z_NEAR[4:6])
    lax.fori_loop(2, 4, build_pair, 0)
    relay(Z_NEAR[6:])
    lax.fori_loop(4, 8, build_pair, 0)

    for step, j in enumerate((0, 1, 3, 2)):
        if j:
            drain(big_x.at[pl.ds(0, NZ * A_ROWS)], ya_recv.at[j])
        drain(big_x.at[pl.ds(0, (NZ - 1) * B_ROWS)], zb_recv.at[j])
        pair_base = lax.rem(y - j + NY, NY) * 2
        for h in range(2):
            q = pair_base + h
            xt_ref[q] = big_x[pl.ds(pl.multiple_of(q * WIDE, WIDE), WIDE), :].T

        def add_pair(pair, _):
            total = None if step == 0 else acc_ref[pair]
            for h in range(2):
                q = pair_base + h
                part = jnp.dot(
                    xt_ref[q], at_ref[pair, pl.ds(pl.multiple_of(q * WIDE, WIDE), WIDE), :],
                    preferred_element_type=F32,
                )
                total = part if total is None else total + part
            if step < NY - 1:
                acc_ref[pair] = total
                return 0
            links = [
                jnp.concatenate(parts, axis=1)
                for parts in zip(group_links(2 * pair), group_links(2 * pair + 1))
            ]
            degree = sum(jnp.sum((part >= 0).astype(F32), axis=0, keepdims=True) for part in links)
            mean = (total / degree).astype(BF)
            mixed = jnp.dot(ws_t, xt_ref[pair], preferred_element_type=F32) + jnp.dot(
                wn_t, mean, preferred_element_type=F32
            )
            coded = mixed.astype(BF)
            ht_ref[2 * pair] = coded[:, :BLK]
            ht_ref[2 * pair + 1] = coded[:, BLK:]
            return 0

        lax.fori_loop(0, 8, add_pair, 0)

    to_scalar.wait()
    block_id = lax.broadcasted_iota(jnp.int32, (R_BLK, BLK), 0)
    lane = lax.broadcasted_iota(jnp.int32, (BLK, BLK), 1)
    neg16 = jnp.full((R_BLK, BLK), NEG, F32)

    def score_block(c, best):
        for m in range(MOST):
            r = row_of(c, m)
            bias = jnp.where(r < 0, NEG, 0.0)
            raw = jnp.dot(th_ref[c], ht_ref[row_at(c, m)], preferred_element_type=F32)
            raw = raw * SCALE + bias
            s_ref[c * MOST + m] = raw
            best = jnp.maximum(best, jnp.where(block_id == r, jnp.max(raw, axis=0, keepdims=True), NEG))
        return best

    top = lax.fori_loop(0, C_LOC, score_block, neg16, unroll=2)
    top_ref[...] = top

    def first_rows(c, total):
        for m in range(MOST):
            r = row_of(c, m)
            high = top_ref[pl.ds(row_at(c, m), 1), :]
            part = jnp.sum(jnp.exp(s_ref[c * MOST + m] - high), axis=0, keepdims=True)
            total = total + jnp.where(block_id == r, part, 0.0)
        return total

    total = lax.fori_loop(0, C_LOC, first_rows, jnp.zeros((R_BLK, BLK), F32), unroll=4)
    rx_ref[0, t] = jnp.where(total > 0.0, top + jnp.log(total), NEG)

    def send_rows(sweep, buf, slot):
        for p in tgt_peers:
            push(buf.at[slot, t], buf.at[slot, t], r_send.at[sweep], r_recv.at[sweep], (s, p))

    def await_rows(sweep, buf, slot):
        drain(buf.at[slot, pl.ds(0, NTGT - 1)], r_recv.at[sweep])
        return buf[slot]

    def send_cols(sweep):
        for p in src_peers:
            push(cx_ref.at[sweep, s], cx_ref.at[sweep, s], c_send.at[sweep], c_recv.at[sweep], (p, t))

    def await_cols(sweep):
        drain(cx_ref.at[sweep, pl.ds(0, NSRC - 1)], c_recv.at[sweep])
        return cx_ref[sweep]

    send_rows(0, rx_ref, 0)

    def probe_slots(block, _):
        table = jnp.broadcast_to(tab_ref[pl.ds(block, 1), :], (8, BLK))
        for half in range(2):
            rows = slice(half * 8, half * 8 + 8)
            which = pp_ref[block, rows, :] // BLK
            sid_ref[block, rows, :] = jnp.take_along_axis(table, which, axis=1)
        return 0

    lax.fori_loop(0, R_BLK, probe_slots, 0)

    def pick(slot, _):
        r = row_at(slot // MOST, lax.rem(slot, MOST))
        for half in range(2):
            rows = slice(half * 8, half * 8 + 8)
            offset = lax.rem(pp_ref[r, rows, :], BLK)
            strip, inner = offset // 8, lax.rem(offset, 8)
            value = jnp.zeros((8, BLK), F32)
            for k in range(BLK // 8):
                got = jnp.take_along_axis(s_ref[slot, k * 8 : k * 8 + 8, :], inner, axis=0)
                value = jnp.where(strip == k, got, value)
            g_ref[slot, rows, :] = jnp.where(sid_ref[r, rows, :] == slot, value, 0.0)
        return 0

    lax.fori_loop(0, SLOTS, pick, 0, unroll=2)

    def merge(block, _):
        total = jnp.zeros((QRY, BLK), F32)
        for c in range(C_LOC):
            total = total + g_ref[jnp.clip(meta_s[block, c], 0, SLOTS)]
        pk_ref[block] = total
        return 0

    lax.fori_loop(0, R_BLK, merge, 0, unroll=4)

    parts = await_rows(0, rx_ref, 0)
    high = jnp.max(parts, axis=0)
    r0 = -(high + jnp.log(jnp.sum(jnp.exp(parts - high[None]), axis=0)))
    r0_ref[...] = r0

    def first_cols(c, carry):
        tops, sums = carry
        shifted = [
            s_ref[c * MOST + m] + r0_ref[pl.ds(row_at(c, m), 1), :]
            for m in range(MOST)
        ]
        high = functools.reduce(jnp.maximum, shifted)
        high = jnp.maximum(jnp.max(high, axis=1, keepdims=True), FLOOR)
        total = jnp.zeros((BLK, BLK), F32)
        for m in range(MOST):
            e = jnp.exp(shifted[m] - high)
            e_ref[c * MOST + m] = e
            total = total + e
        total = jnp.sum(total, axis=1, keepdims=True)
        return jnp.where(lane == c, high, tops), jnp.where(lane == c, total, sums)

    zero_tile = jnp.zeros((BLK, BLK), F32)
    tops, sums = lax.fori_loop(0, C_LOC, first_cols, (zero_tile, zero_tile), unroll=2)
    tops = tops.T[:C_LOC]
    sums = sums.T[:C_LOC]
    cx_ref[0, s] = jnp.where(sums > 0.0, tops + jnp.log(sums), NEG)
    send_cols(0)
    parts = await_cols(0)
    high = jnp.max(parts, axis=0)
    share = R_BLK * BLK * NSRC / (C_LOC * BLK * NTGT)
    c0 = math.log(share) - (high + jnp.log(jnp.sum(jnp.exp(parts - high[None]), axis=0)))
    factor = jnp.exp(tops + c0)

    def spread(weights):
        upright = jnp.concatenate([weights, jnp.zeros((BLK - C_LOC, BLK), F32)], axis=0).T
        for c in range(C_LOC):
            wb_ref[c] = jnp.broadcast_to(upright[:, c : c + 1], (BLK, BLK))

    def sweep_body(sweep, carry, rows_buf):
        _, col_scale = carry
        spread(factor * col_scale)

        def rows_of(c, total):
            for m in range(MOST):
                part = jnp.sum(e_ref[c * MOST + m] * wb_ref[c], axis=0, keepdims=True)
                total = total + jnp.where(block_id == row_of(c, m), part, 0.0)
            return total

        total = lax.fori_loop(0, C_LOC, rows_of, jnp.zeros((R_BLK, BLK), F32), unroll=4)
        slot = 1 if rows_buf is rx_ref else sweep - 1
        rows_buf[slot, t] = total.astype(rows_buf.dtype)
        send_rows(sweep, rows_buf, slot)
        parts = await_rows(sweep, rows_buf, slot)
        row_scale = 1.0 / jnp.sum(parts.astype(F32), axis=0)
        u_ref[...] = row_scale

        def cols_of(c, sums):
            total = jnp.zeros((BLK, BLK), F32)
            for m in range(MOST):
                r = row_at(c, m)
                total = total + e_ref[c * MOST + m] * u_ref[pl.ds(r, 1), :]
            return jnp.where(lane == c, jnp.sum(total, axis=1, keepdims=True), sums)

        sums = lax.fori_loop(0, C_LOC, cols_of, zero_tile, unroll=4).T[:C_LOC]
        cx_ref[sweep, s] = sums * factor
        send_cols(sweep)
        return row_scale, share / jnp.sum(await_cols(sweep), axis=0)

    scales = (jnp.ones((R_BLK, BLK), F32), jnp.ones((C_LOC, BLK), F32))
    scales = lax.fori_loop(1, SWEEPS - 1, lambda i, carry: sweep_body(i, carry, rh_ref), scales)
    row_scale, col_scale = sweep_body(SWEEPS - 1, scales, rx_ref)
    row_pot = r0 + jnp.log(row_scale)
    col_pot = c0 + jnp.log(col_scale) + math.log(CAND * BLK)
    u_ref[...] = row_pot
    top_ref[:C_LOC, :] = col_pot
    lane8 = lax.broadcasted_iota(jnp.int32, (8, BLK), 1)

    def finish(block, _):
        done = []
        for half in range(2):
            rows = slice(half * 8, half * 8 + 8)
            sid = sid_ref[block, rows, :]
            offset = lax.rem(pp_ref[block, rows, :], BLK)
            owner = sid // MOST
            value = jnp.zeros((8, BLK), F32)
            for c in range(C_LOC):
                strip = jnp.broadcast_to(top_ref[c : c + 1, :], (8, BLK))
                value = jnp.where(owner == c, jnp.take_along_axis(strip, offset, axis=1), value)
            value = value + pk_ref[block, rows, :] + u_ref[pl.ds(block, 1), :]
            done.append(jnp.where(sid >= 0, value, 0.0))
        low, high = done
        fs_ref[2 * block] = jnp.where(lane8 < ROWS, low, pltpu.roll(high, ROWS, 1))
        fs_ref[2 * block + 1] = jnp.where(lane8 < ROWS, pltpu.roll(low, ROWS, 1), high)
        return 0

    lax.fori_loop(0, R_BLK, finish, 0, unroll=4)
    for p in tgt_peers:
        push(fs_ref.at[p], fr_ref.at[t], f_send, f_recv, (s, p))
    fr_ref[t] = fs_ref[t]
    drain(fr_ref.at[pl.ds(0, NTGT - 1)], f_recv)
    out_ref[...] = jnp.sum(fr_ref[...], axis=0)

    drain(big_x.at[pl.ds(0, 7 * A_ROWS)], a_send)
    drain(big_x.at[pl.ds(0, 3 * B_ROWS)], b_send)
    drain(big_x.at[pl.ds(0, 24 * A_ROWS)], ya_send)
    drain(big_x.at[pl.ds(0, 28 * B_ROWS)], zb_send)
    drain(lk_ref.at[pl.ds(0, NTGT - 1)], lk_send)
    for sweep in range(SWEEPS):
        rows_sent = rh_ref.at[sweep - 1] if 0 < sweep < SWEEPS - 1 else rx_ref.at[min(sweep, 1)]
        drain(rows_sent.at[pl.ds(0, NTGT - 1)], r_send.at[sweep])
        drain(cx_ref.at[sweep, pl.ds(0, NSRC - 1)], c_send.at[sweep])
    drain(fs_ref.at[pl.ds(0, NTGT - 1)], f_send)


def shards(
    source_embed,
    source_links,
    source_degree,
    target_embed,
    target_links,
    target_degree,
    w_self,
    w_neigh,
    cand_blocks,
    probe_pairs,
):
    vmem = pl.BlockSpec(memory_space=pltpu.VMEM)
    hbm = pl.BlockSpec(memory_space=pltpu.HBM)
    dma = pltpu.SemaphoreType.DMA
    packed = pl.pallas_call(
        sinkhorn_kernel,
        out_shape=jax.ShapeDtypeStruct((8, BLK), F32),
        in_specs=[hbm] * 10,
        out_specs=vmem,
        scratch_shapes=[
            pltpu.VMEM((KMAX, ROWS), jnp.int32),
            pltpu.VMEM((1, ROWS), jnp.int32),
            pltpu.VMEM((C_LOC * BLK, D), BF),
            pltpu.VMEM((KMAX, C_LOC * BLK), jnp.int32),
            pltpu.VMEM((1, C_LOC * BLK), jnp.int32),
            pltpu.VMEM((D, D), BF),
            pltpu.VMEM((D, D), BF),
            pltpu.VMEM((R_BLK, CAND), jnp.int32),
            pltpu.VMEM((QRY, R_BLK * BLK), jnp.int32),
            pltpu.VMEM((R_BLK, BLK), jnp.int32),
            pltpu.VMEM((R_BLK, QRY, BLK), jnp.int32),
            pltpu.VMEM((R_BLK + 8, BLK), jnp.int32),
            pltpu.SMEM((R_BLK + 8, BLK), jnp.int32),
            pltpu.VMEM((8, D, WIDE), F32),
            dma((10,)),
            dma,
            pltpu.VMEM((WIDE // 16, 16, BLK), jnp.int16),
            pltpu.VMEM((NTGT * ROWS, D), BF),
            pltpu.VMEM((8, D, WIDE), BF),
            pltpu.VMEM((NTGT, KMAX // 2, BLK), jnp.int32),
            pltpu.VMEM((8, NTGT * ROWS, WIDE), BF),
            pltpu.VMEM((R_BLK, D, BLK), BF),
            pltpu.VMEM((D, C_LOC * BLK), BF),
            pltpu.VMEM((C_LOC * BLK, WIDE), BF),
            pltpu.VMEM((C_LOC, BLK, D), BF),
            pltpu.VMEM((SLOTS, BLK, BLK), F32),
            pltpu.VMEM((SLOTS, BLK, BLK), F32),
            pltpu.VMEM((C_LOC, BLK, BLK), F32),
            pltpu.VMEM((2, NTGT, R_BLK, BLK), F32),
            pltpu.VMEM((SWEEPS - 2, NTGT, R_BLK, BLK), BF),
            pltpu.VMEM((SWEEPS, NSRC, C_LOC, BLK), F32),
            pltpu.VMEM((R_BLK, BLK), F32),
            pltpu.VMEM((R_BLK, BLK), F32),
            pltpu.VMEM((R_BLK, BLK), F32),
            pltpu.VMEM((R_BLK, QRY, BLK), jnp.int32),
            pltpu.VMEM((SLOTS + 1, QRY, BLK), F32),
            pltpu.VMEM((R_BLK, QRY, BLK), F32),
            pltpu.VMEM((NTGT, 8, BLK), F32),
            pltpu.VMEM((NTGT, 8, BLK), F32),
            dma, dma((NZ,)), dma, dma((NY,)), dma, dma((NY,)), dma, dma((NY,)), dma, dma,
            dma((SWEEPS,)), dma((SWEEPS,)), dma((SWEEPS,)), dma((SWEEPS,)), dma, dma,
        ],
        compiler_params=pltpu.CompilerParams(
            collective_id=0, has_side_effects=True, vmem_limit_bytes=64 * 2**20
        ),
    )(
        source_embed, source_links.T, source_degree.reshape(1, -1), target_embed, target_links.T,
        target_degree.reshape(1, -1), w_self, w_neigh, cand_blocks, probe_pairs.T,
    )
    return packed.reshape(8, 2, ROWS).transpose(2, 1, 0).reshape(ROWS, QRY)


def solution(mesh):
    placed = (
        P(("src", "tgt"), None),
        P(("src", "tgt"), None),
        P(("src", "tgt")),
        P("tgt", None),
        P("tgt", None),
        P("tgt"),
        P(),
        P(),
        P("src", None),
        P("src", None),
    )
    return jax.shard_map(
        shards, mesh=mesh, in_specs=placed, out_specs=P(("src", "tgt"), None), check_vma=False
    )
```

```python
import functools
import math

import jax
import jax.numpy as jnp
from jax import lax
from jax.experimental import pallas as pl
from jax.experimental.pallas import tpu as pltpu
from jax.sharding import PartitionSpec as P

D = 256
BLK = 128
CAND = 32
MOST = 4
QRY = 16
SWEEPS = 4
KMAX = 8
NY, NZ = 4, 8
NSRC, NTGT = 8, 32
ROWS = 64
R_BLK = 16
C_LOC = 8
SLOTS = C_LOC * MOST
A_ROWS = 48
B_ROWS = 16
WIDE = 256
NEG = -1e30
FLOOR = -1e29
SCALE = 3.0 / math.sqrt(D)
MESH = pl.DeviceIdType.MESH
BF = jnp.bfloat16
F32 = jnp.float32


def far_first():
    offs = [(dy, dz) for dy in range(NY) for dz in range(NZ) if (dy, dz) != (0, 0)]
    dist = lambda o: min(o[0], NY - o[0]) + min(o[1], NZ - o[1])
    return sorted(offs, key=lambda o: (-dist(o), o))


Z_FAR = (4, 3, 5, 2, 6, 1, 7)
Z_NEAR = (1, 7, 2, 6, 3, 5, 4)
Y_FAR = (2, 1, 3)


def sinkhorn_kernel(
    x_hbm, sl_hbm, sd_hbm, t_hbm, tl_hbm, td_hbm, ws_hbm, wn_hbm, cand_hbm, pp_hbm,
    out_ref,
    sl_ref, sd_ref, t_ref, tl_ref, td_ref, ws_ref, wn_ref, cand_ref, pq_ref,
    tab_ref, pp_ref, meta_ref, meta_s, acc_ref, in_sem, meta_sem,
    iota_ref, big_x, xt_ref, lk_ref, at_ref, ht_ref, tt_ref, att_ref, th_ref,
    s_ref, e_ref, wb_ref, rx_ref, rh_ref, cx_ref, top_ref, r0_ref, u_ref, sid_ref, g_ref, pk_ref,
    fs_ref, fr_ref,
    a_send, a_recv, b_send, b_recv, ya_send, ya_recv, zb_send, zb_recv, lk_send, lk_recv,
    r_send, r_recv, c_send, c_recv, f_send, f_recv,
):
    s = lax.axis_index("src")
    t = lax.axis_index("tgt")
    y = t // NZ
    z = lax.rem(t, NZ)
    tgt_peers = [lax.rem(y + dy, NY) * NZ + lax.rem(z + dz, NZ) for dy, dz in far_first()]
    sx = s // 2
    score = lax.rem(s, 2)
    src_peers = [
        lax.rem(sx + dx, 4) * 2 + (score if same else 1 - score)
        for dx, same in ((2, False), (2, True), (1, False), (3, False), (1, True), (3, True), (0, False))
    ]

    staged = (
        (sl_hbm, sl_ref), (sd_hbm, sd_ref), (cand_hbm, cand_ref), (tl_hbm, tl_ref), (td_hbm, td_ref),
        (t_hbm, t_ref), (ws_hbm, ws_ref), (wn_hbm, wn_ref), (pp_hbm, pq_ref),
        (x_hbm, big_x.at[pl.ds(t * ROWS, ROWS)]),
    )
    loads = [pltpu.make_async_copy(src, dst, in_sem.at[i]) for i, (src, dst) in enumerate(staged)]
    for load in loads:
        load.start()

    barrier = pltpu.get_barrier_semaphore()
    for p in tgt_peers:
        pl.semaphore_signal(barrier, inc=1, device_id=(s, p), device_id_type=MESH)
    for p in src_peers:
        pl.semaphore_signal(barrier, inc=1, device_id=(p, t), device_id_type=MESH)

    tile_rows = lax.broadcasted_iota(jnp.int32, (WIDE // 16, 16, BLK), 0) * 16
    tile_rows = tile_rows + lax.broadcasted_iota(jnp.int32, (WIDE // 16, 16, BLK), 1)
    iota_ref[...] = tile_rows.astype(jnp.int16)
    lane4 = lax.broadcasted_iota(jnp.int32, (KMAX // 2, BLK), 1)
    loads[0].wait()
    loads[1].wait()
    slot8 = lax.broadcasted_iota(jnp.int32, (KMAX, ROWS), 0)
    own = jnp.where(slot8 < sd_ref[...], sl_ref[...], -1)
    own = jnp.concatenate([own, own], axis=1)
    lk_ref[t] = jnp.where(lane4 < ROWS, own[:4], own[4:])

    loads[2].wait()
    local = cand_ref[...] - t * C_LOC
    local = jnp.concatenate([local, jnp.full((R_BLK, BLK - CAND), -1, jnp.int32)], axis=1)
    lane16 = lax.broadcasted_iota(jnp.int32, (R_BLK, BLK), 1)
    row16 = lax.broadcasted_iota(jnp.int32, (R_BLK, BLK), 0)
    hits = jnp.zeros((R_BLK, BLK), jnp.int32)
    for c in range(C_LOC):
        named = jnp.max(jnp.where(local == c, 1, 0), axis=1, keepdims=True)
        hits = jnp.where(lane16 == c, named, hits)
    before = jnp.zeros((R_BLK, BLK), jnp.int32)
    for r in range(R_BLK - 1):
        before = before + jnp.where(row16 > r, hits[r : r + 1, :], 0)
    place = jnp.where(hits > 0, lane16 * MOST + before, SLOTS)
    meta_ref[:R_BLK, :] = place
    rows_of_slot = [
        jnp.sum(
            jnp.where((hits > 0) & (before == m), row16 + 1, 0), axis=0, keepdims=True
        )
        for m in range(MOST)
    ]
    pad4 = jnp.zeros((8 - MOST, BLK), jnp.int32)
    meta_ref[R_BLK:, :] = jnp.concatenate(rows_of_slot + [pad4], axis=0) - 1
    table = jnp.full((R_BLK, BLK), -1, jnp.int32)
    for c in range(C_LOC):
        table = jnp.where(local == c, jnp.broadcast_to(place[:, c : c + 1], (R_BLK, BLK)), table)
    tab_ref[...] = table
    to_scalar = pltpu.make_async_copy(meta_ref, meta_s, meta_sem)
    to_scalar.start()

    def row_of(c, m):
        return meta_s[R_BLK + m, c]

    def row_at(c, m):
        return jnp.clip(row_of(c, m), 0, R_BLK - 1)

    g_ref[SLOTS] = jnp.zeros((QRY, BLK), F32)

    for load in loads[3:]:
        load.wait()
    for block in range(R_BLK):
        pp_ref[block] = pq_ref[:, block * BLK : (block + 1) * BLK]
    ws_t = ws_ref[...].T
    wn_t = wn_ref[...].T
    for chunk in range(4):
        tt_ref[:, chunk * WIDE : (chunk + 1) * WIDE] = t_ref[chunk * WIDE : (chunk + 1) * WIDE, :].T

    def build(links, chunks, put):
        singles = [part[k : k + 1, :] for part in links for k in range(part.shape[0])]
        rows, counts = [], []
        for part in links:
            count = jnp.zeros(part.shape, F32)
            for single in singles:
                count = count + jnp.where(part == single, 1.0, 0.0)
            counts += [
                jnp.broadcast_to(count[k : k + 1, :], (16, BLK)).astype(BF) for k in range(part.shape[0])
            ]
        for single in singles:
            rows.append(jnp.broadcast_to(single, (16, BLK)).astype(jnp.int16))

        def body(q, _):
            base = jnp.full((16, BLK), q * WIDE, jnp.int32).astype(jnp.int16)
            total = jnp.zeros((WIDE // 16, 16, BLK), BF)
            for k in range(KMAX):
                total = jnp.where((rows[k] - base)[None] == iota_ref[...], counts[k][None], total)
            put(q, total.reshape(WIDE, BLK))
            return 0

        lax.fori_loop(0, chunks, body, 0)

    def encode(table_t, adjacency, own_t, degree):
        total = jnp.dot(table_t, adjacency, preferred_element_type=F32)
        mean = (total / degree).astype(BF)
        mixed = jnp.dot(ws_t, own_t, preferred_element_type=F32) + jnp.dot(
            wn_t, mean, preferred_element_type=F32
        )
        return mixed.astype(BF)

    for chunk in range(4):
        cols = slice(chunk * WIDE, (chunk + 1) * WIDE)
        degree = td_ref[:, cols]
        slot_rows = lax.broadcasted_iota(jnp.int32, (KMAX, WIDE), 0)
        links = jnp.where(slot_rows < degree, tl_ref[:, cols], -1)
        degree = degree.astype(F32)
        for half in range(2):
            def put(q, value, half=half):
                att_ref[pl.ds(q * WIDE, WIDE), half * BLK : (half + 1) * BLK] = value

            build([links[:, half * BLK : (half + 1) * BLK]], 4, put)
        coded = encode(tt_ref[...], att_ref[...], tt_ref[:, cols], degree).T
        th_ref[2 * chunk] = coded[:BLK]
        th_ref[2 * chunk + 1] = coded[BLK:]

    pl.semaphore_wait(barrier, NTGT - 1 + NSRC - 1)

    def push(src, dst, ssem, rsem, dev):
        pltpu.make_async_remote_copy(
            src_ref=src, dst_ref=dst, send_sem=ssem, recv_sem=rsem, device_id=dev, device_id_type=MESH
        ).start()

    def drain(ref, sem):
        pltpu.make_async_copy(ref, ref, sem).wait()

    def part_a(d):
        return big_x.at[pl.ds(d * ROWS, A_ROWS)]

    def part_b(d):
        return big_x.at[pl.ds(d * ROWS + A_ROWS, B_ROWS)]

    def at_yz(dy, dz):
        return lax.rem(y + dy + NY, NY) * NZ + lax.rem(z + dz + NZ, NZ)

    for p in tgt_peers:
        push(lk_ref.at[t], lk_ref.at[t], lk_send, lk_recv, (s, p))
    for k in Z_FAR:
        push(part_a(t), part_a(t), a_send, a_recv.at[k], (s, at_yz(0, k)))
    for j in Y_FAR:
        push(part_b(t), part_b(t), b_send, b_recv.at[j], (s, at_yz(j, 0)))
    for j in Y_FAR:
        push(part_a(t), part_a(t), ya_send, ya_recv.at[j], (s, at_yz(j, 0)))
    for k in Z_FAR:
        push(part_b(t), part_b(t), zb_send, zb_recv.at[0], (s, at_yz(0, k)))

    for j in Y_FAR[::-1]:
        drain(part_b(t), b_recv.at[j])
        d = at_yz(-j, 0)
        for k in Z_FAR:
            push(part_b(d), part_b(d), zb_send, zb_recv.at[j], (s, at_yz(0, k)))
    def relay(near):
        for k in near:
            drain(part_a(t), a_recv.at[k])
            d = at_yz(0, -k)
            for j in Y_FAR:
                push(part_a(d), part_a(d), ya_send, ya_recv.at[j], (s, at_yz(j, 0)))

    relay(Z_NEAR[:4])
    drain(lk_ref.at[pl.ds(0, NTGT - 1)], lk_recv)

    def group_links(block):
        first, second = lk_ref[2 * block], lk_ref[2 * block + 1]
        return [
            jnp.where(lane4 < ROWS, first, pltpu.roll(second, ROWS, 1)),
            jnp.where(lane4 < ROWS, pltpu.roll(first, ROWS, 1), second),
        ]

    def build_pair(pair, _):
        for half in range(2):
            def put(q, value, half=half):
                at_ref[pair, pl.ds(q * WIDE, WIDE), half * BLK : (half + 1) * BLK] = value

            build(group_links(2 * pair + half), 8, put)
        return 0

    lax.fori_loop(0, 2, build_pair, 0)
    relay(Z_NEAR[4:6])
    lax.fori_loop(2, 4, build_pair, 0)
    relay(Z_NEAR[6:])
    lax.fori_loop(4, 8, build_pair, 0)

    for step, j in enumerate((0, 1, 3, 2)):
        if j:
            drain(big_x.at[pl.ds(0, NZ * A_ROWS)], ya_recv.at[j])
        drain(big_x.at[pl.ds(0, (NZ - 1) * B_ROWS)], zb_recv.at[j])
        pair_base = lax.rem(y - j + NY, NY) * 2
        for h in range(2):
            q = pair_base + h
            xt_ref[q] = big_x[pl.ds(pl.multiple_of(q * WIDE, WIDE), WIDE), :].T

        def add_pair(pair, _):
            total = None if step == 0 else acc_ref[pair]
            for h in range(2):
                q = pair_base + h
                part = jnp.dot(
                    xt_ref[q], at_ref[pair, pl.ds(pl.multiple_of(q * WIDE, WIDE), WIDE), :],
                    preferred_element_type=F32,
                )
                total = part if total is None else total + part
            if step < NY - 1:
                acc_ref[pair] = total
                return 0
            links = [
                jnp.concatenate(parts, axis=1)
                for parts in zip(group_links(2 * pair), group_links(2 * pair + 1))
            ]
            degree = sum(jnp.sum((part >= 0).astype(F32), axis=0, keepdims=True) for part in links)
            mean = (total / degree).astype(BF)
            mixed = jnp.dot(ws_t, xt_ref[pair], preferred_element_type=F32) + jnp.dot(
                wn_t, mean, preferred_element_type=F32
            )
            coded = mixed.astype(BF)
            ht_ref[2 * pair] = coded[:, :BLK]
            ht_ref[2 * pair + 1] = coded[:, BLK:]
            return 0

        lax.fori_loop(0, 8, add_pair, 0, unroll=4)

    to_scalar.wait()
    block_id = lax.broadcasted_iota(jnp.int32, (R_BLK, BLK), 0)
    lane = lax.broadcasted_iota(jnp.int32, (BLK, BLK), 1)
    neg16 = jnp.full((R_BLK, BLK), NEG, F32)

    def score_block(c, best):
        for m in range(MOST):
            r = row_of(c, m)
            bias = jnp.where(r < 0, NEG, 0.0)
            raw = jnp.dot(th_ref[c], ht_ref[row_at(c, m)], preferred_element_type=F32)
            raw = raw * SCALE + bias
            s_ref[c * MOST + m] = raw
            best = jnp.maximum(best, jnp.where(block_id == r, jnp.max(raw, axis=0, keepdims=True), NEG))
        return best

    top = lax.fori_loop(0, C_LOC, score_block, neg16, unroll=2)
    top_ref[...] = top

    def first_rows(c, total):
        for m in range(MOST):
            r = row_of(c, m)
            high = top_ref[pl.ds(row_at(c, m), 1), :]
            part = jnp.sum(jnp.exp(s_ref[c * MOST + m] - high), axis=0, keepdims=True)
            total = total + jnp.where(block_id == r, part, 0.0)
        return total

    total = lax.fori_loop(0, C_LOC, first_rows, jnp.zeros((R_BLK, BLK), F32), unroll=4)
    rx_ref[0, t] = jnp.where(total > 0.0, top + jnp.log(total), NEG)

    def send_rows(sweep, buf, slot):
        for p in tgt_peers:
            push(buf.at[slot, t], buf.at[slot, t], r_send.at[sweep], r_recv.at[sweep], (s, p))

    def await_rows(sweep, buf, slot):
        drain(buf.at[slot, pl.ds(0, NTGT - 1)], r_recv.at[sweep])
        return buf[slot]

    def send_cols(sweep):
        for p in src_peers:
            push(cx_ref.at[sweep, s], cx_ref.at[sweep, s], c_send.at[sweep], c_recv.at[sweep], (p, t))

    def await_cols(sweep):
        drain(cx_ref.at[sweep, pl.ds(0, NSRC - 1)], c_recv.at[sweep])
        return cx_ref[sweep]

    send_rows(0, rx_ref, 0)

    def probe_slots(block, _):
        table = jnp.broadcast_to(tab_ref[pl.ds(block, 1), :], (8, BLK))
        for half in range(2):
            rows = slice(half * 8, half * 8 + 8)
            which = pp_ref[block, rows, :] // BLK
            sid_ref[block, rows, :] = jnp.take_along_axis(table, which, axis=1)
        return 0

    lax.fori_loop(0, R_BLK, probe_slots, 0)

    def pick(slot, _):
        r = row_at(slot // MOST, lax.rem(slot, MOST))
        for half in range(2):
            rows = slice(half * 8, half * 8 + 8)
            offset = lax.rem(pp_ref[r, rows, :], BLK)
            strip, inner = offset // 8, lax.rem(offset, 8)
            value = jnp.zeros((8, BLK), F32)
            for k in range(BLK // 8):
                got = jnp.take_along_axis(s_ref[slot, k * 8 : k * 8 + 8, :], inner, axis=0)
                value = jnp.where(strip == k, got, value)
            g_ref[slot, rows, :] = jnp.where(sid_ref[r, rows, :] == slot, value, 0.0)
        return 0

    lax.fori_loop(0, SLOTS, pick, 0, unroll=2)

    def merge(block, _):
        total = jnp.zeros((QRY, BLK), F32)
        for c in range(C_LOC):
            total = total + g_ref[jnp.clip(meta_s[block, c], 0, SLOTS)]
        pk_ref[block] = total
        return 0

    lax.fori_loop(0, R_BLK, merge, 0, unroll=4)

    parts = await_rows(0, rx_ref, 0)
    high = jnp.max(parts, axis=0)
    r0 = -(high + jnp.log(jnp.sum(jnp.exp(parts - high[None]), axis=0)))
    r0_ref[...] = r0

    def first_cols(c, carry):
        tops, sums = carry
        shifted = [
            s_ref[c * MOST + m] + r0_ref[pl.ds(row_at(c, m), 1), :]
            for m in range(MOST)
        ]
        high = functools.reduce(jnp.maximum, shifted)
        high = jnp.maximum(jnp.max(high, axis=1, keepdims=True), FLOOR)
        total = jnp.zeros((BLK, BLK), F32)
        for m in range(MOST):
            e = jnp.exp(shifted[m] - high)
            e_ref[c * MOST + m] = e
            total = total + e
        total = jnp.sum(total, axis=1, keepdims=True)
        return jnp.where(lane == c, high, tops), jnp.where(lane == c, total, sums)

    zero_tile = jnp.zeros((BLK, BLK), F32)
    tops, sums = lax.fori_loop(0, C_LOC, first_cols, (zero_tile, zero_tile), unroll=4)
    tops = tops.T[:C_LOC]
    sums = sums.T[:C_LOC]
    cx_ref[0, s] = jnp.where(sums > 0.0, tops + jnp.log(sums), NEG)
    send_cols(0)
    parts = await_cols(0)
    high = jnp.max(parts, axis=0)
    share = R_BLK * BLK * NSRC / (C_LOC * BLK * NTGT)
    c0 = math.log(share) - (high + jnp.log(jnp.sum(jnp.exp(parts - high[None]), axis=0)))
    factor = jnp.exp(tops + c0)

    def spread(weights):
        upright = jnp.concatenate([weights, jnp.zeros((BLK - C_LOC, BLK), F32)], axis=0).T
        for c in range(C_LOC):
            wb_ref[c] = jnp.broadcast_to(upright[:, c : c + 1], (BLK, BLK))

    def sweep_body(sweep, carry, rows_buf):
        _, col_scale = carry
        spread(factor * col_scale)

        def rows_of(c, total):
            for m in range(MOST):
                part = jnp.sum(e_ref[c * MOST + m] * wb_ref[c], axis=0, keepdims=True)
                total = total + jnp.where(block_id == row_of(c, m), part, 0.0)
            return total

        total = lax.fori_loop(0, C_LOC, rows_of, jnp.zeros((R_BLK, BLK), F32), unroll=8)
        slot = 1 if rows_buf is rx_ref else sweep - 1
        rows_buf[slot, t] = total.astype(rows_buf.dtype)
        send_rows(sweep, rows_buf, slot)
        parts = await_rows(sweep, rows_buf, slot)
        row_scale = 1.0 / jnp.sum(parts.astype(F32), axis=0)
        u_ref[...] = row_scale

        def cols_of(c, sums):
            total = jnp.zeros((BLK, BLK), F32)
            for m in range(MOST):
                r = row_at(c, m)
                total = total + e_ref[c * MOST + m] * u_ref[pl.ds(r, 1), :]
            return jnp.where(lane == c, jnp.sum(total, axis=1, keepdims=True), sums)

        sums = lax.fori_loop(0, C_LOC, cols_of, zero_tile, unroll=8).T[:C_LOC]
        cx_ref[sweep, s] = sums * factor
        send_cols(sweep)
        return row_scale, share / jnp.sum(await_cols(sweep), axis=0)

    scales = (jnp.ones((R_BLK, BLK), F32), jnp.ones((C_LOC, BLK), F32))
    scales = lax.fori_loop(1, SWEEPS - 1, lambda i, carry: sweep_body(i, carry, rh_ref), scales)
    row_scale, col_scale = sweep_body(SWEEPS - 1, scales, rx_ref)
    row_pot = r0 + jnp.log(row_scale)
    col_pot = c0 + jnp.log(col_scale) + math.log(CAND * BLK)
    u_ref[...] = row_pot
    top_ref[:C_LOC, :] = col_pot
    lane8 = lax.broadcasted_iota(jnp.int32, (8, BLK), 1)

    def finish(block, _):
        done = []
        for half in range(2):
            rows = slice(half * 8, half * 8 + 8)
            sid = sid_ref[block, rows, :]
            offset = lax.rem(pp_ref[block, rows, :], BLK)
            owner = sid // MOST
            value = jnp.zeros((8, BLK), F32)
            for c in range(C_LOC):
                strip = jnp.broadcast_to(top_ref[c : c + 1, :], (8, BLK))
                value = jnp.where(owner == c, jnp.take_along_axis(strip, offset, axis=1), value)
            value = value + pk_ref[block, rows, :] + u_ref[pl.ds(block, 1), :]
            done.append(jnp.where(sid >= 0, value, 0.0))
        low, high = done
        fs_ref[2 * block] = jnp.where(lane8 < ROWS, low, pltpu.roll(high, ROWS, 1))
        fs_ref[2 * block + 1] = jnp.where(lane8 < ROWS, pltpu.roll(low, ROWS, 1), high)
        return 0

    lax.fori_loop(0, R_BLK, finish, 0, unroll=4)
    for p in tgt_peers:
        push(fs_ref.at[p], fr_ref.at[t], f_send, f_recv, (s, p))
    fr_ref[t] = fs_ref[t]
    drain(fr_ref.at[pl.ds(0, NTGT - 1)], f_recv)
    out_ref[...] = jnp.sum(fr_ref[...], axis=0)

    drain(big_x.at[pl.ds(0, 7 * A_ROWS)], a_send)
    drain(big_x.at[pl.ds(0, 3 * B_ROWS)], b_send)
    drain(big_x.at[pl.ds(0, 24 * A_ROWS)], ya_send)
    drain(big_x.at[pl.ds(0, 28 * B_ROWS)], zb_send)
    drain(lk_ref.at[pl.ds(0, NTGT - 1)], lk_send)
    for sweep in range(SWEEPS):
        rows_sent = rh_ref.at[sweep - 1] if 0 < sweep < SWEEPS - 1 else rx_ref.at[min(sweep, 1)]
        drain(rows_sent.at[pl.ds(0, NTGT - 1)], r_send.at[sweep])
        drain(cx_ref.at[sweep, pl.ds(0, NSRC - 1)], c_send.at[sweep])
    drain(fs_ref.at[pl.ds(0, NTGT - 1)], f_send)


def shards(
    source_embed,
    source_links,
    source_degree,
    target_embed,
    target_links,
    target_degree,
    w_self,
    w_neigh,
    cand_blocks,
    probe_pairs,
):
    vmem = pl.BlockSpec(memory_space=pltpu.VMEM)
    hbm = pl.BlockSpec(memory_space=pltpu.HBM)
    dma = pltpu.SemaphoreType.DMA
    packed = pl.pallas_call(
        sinkhorn_kernel,
        out_shape=jax.ShapeDtypeStruct((8, BLK), F32),
        in_specs=[hbm] * 10,
        out_specs=vmem,
        scratch_shapes=[
            pltpu.VMEM((KMAX, ROWS), jnp.int32),
            pltpu.VMEM((1, ROWS), jnp.int32),
            pltpu.VMEM((C_LOC * BLK, D), BF),
            pltpu.VMEM((KMAX, C_LOC * BLK), jnp.int32),
            pltpu.VMEM((1, C_LOC * BLK), jnp.int32),
            pltpu.VMEM((D, D), BF),
            pltpu.VMEM((D, D), BF),
            pltpu.VMEM((R_BLK, CAND), jnp.int32),
            pltpu.VMEM((QRY, R_BLK * BLK), jnp.int32),
            pltpu.VMEM((R_BLK, BLK), jnp.int32),
            pltpu.VMEM((R_BLK, QRY, BLK), jnp.int32),
            pltpu.VMEM((R_BLK + 8, BLK), jnp.int32),
            pltpu.SMEM((R_BLK + 8, BLK), jnp.int32),
            pltpu.VMEM((8, D, WIDE), F32),
            dma((10,)),
            dma,
            pltpu.VMEM((WIDE // 16, 16, BLK), jnp.int16),
            pltpu.VMEM((NTGT * ROWS, D), BF),
            pltpu.VMEM((8, D, WIDE), BF),
            pltpu.VMEM((NTGT, KMAX // 2, BLK), jnp.int32),
            pltpu.VMEM((8, NTGT * ROWS, WIDE), BF),
            pltpu.VMEM((R_BLK, D, BLK), BF),
            pltpu.VMEM((D, C_LOC * BLK), BF),
            pltpu.VMEM((C_LOC * BLK, WIDE), BF),
            pltpu.VMEM((C_LOC, BLK, D), BF),
            pltpu.VMEM((SLOTS, BLK, BLK), F32),
            pltpu.VMEM((SLOTS, BLK, BLK), F32),
            pltpu.VMEM((C_LOC, BLK, BLK), F32),
            pltpu.VMEM((2, NTGT, R_BLK, BLK), F32),
            pltpu.VMEM((SWEEPS - 2, NTGT, R_BLK, BLK), BF),
            pltpu.VMEM((SWEEPS, NSRC, C_LOC, BLK), F32),
            pltpu.VMEM((R_BLK, BLK), F32),
            pltpu.VMEM((R_BLK, BLK), F32),
            pltpu.VMEM((R_BLK, BLK), F32),
            pltpu.VMEM((R_BLK, QRY, BLK), jnp.int32),
            pltpu.VMEM((SLOTS + 1, QRY, BLK), F32),
            pltpu.VMEM((R_BLK, QRY, BLK), F32),
            pltpu.VMEM((NTGT, 8, BLK), F32),
            pltpu.VMEM((NTGT, 8, BLK), F32),
            dma, dma((NZ,)), dma, dma((NY,)), dma, dma((NY,)), dma, dma((NY,)), dma, dma,
            dma((SWEEPS,)), dma((SWEEPS,)), dma((SWEEPS,)), dma((SWEEPS,)), dma, dma,
        ],
        compiler_params=pltpu.CompilerParams(
            collective_id=0, has_side_effects=True, vmem_limit_bytes=64 * 2**20
        ),
    )(
        source_embed, source_links.T, source_degree.reshape(1, -1), target_embed, target_links.T,
        target_degree.reshape(1, -1), w_self, w_neigh, cand_blocks, probe_pairs.T,
    )
    return packed.reshape(8, 2, ROWS).transpose(2, 1, 0).reshape(ROWS, QRY)


def solution(mesh):
    placed = (
        P(("src", "tgt"), None),
        P(("src", "tgt"), None),
        P(("src", "tgt")),
        P("tgt", None),
        P("tgt", None),
        P("tgt"),
        P(),
        P(),
        P("src", None),
        P("src", None),
    )
    return jax.shard_map(
        shards, mesh=mesh, in_specs=placed, out_specs=P(("src", "tgt"), None), check_vma=False
    )
```

```python
import functools
import math

import jax
import jax.numpy as jnp
from jax import lax
from jax.experimental import pallas as pl
from jax.experimental.pallas import tpu as pltpu
from jax.sharding import PartitionSpec as P

D = 256
BLK = 128
CAND = 32
MOST = 4
QRY = 16
SWEEPS = 4
KMAX = 8
NY, NZ = 4, 8
NSRC, NTGT = 8, 32
ROWS = 64
R_BLK = 16
C_LOC = 8
SLOTS = C_LOC * MOST
A_ROWS = 48
B_ROWS = 16
WIDE = 256
NEG = -1e30
FLOOR = -1e29
SCALE = 3.0 / math.sqrt(D)
MESH = pl.DeviceIdType.MESH
BF = jnp.bfloat16
F32 = jnp.float32


def far_first():
    offs = [(dy, dz) for dy in range(NY) for dz in range(NZ) if (dy, dz) != (0, 0)]
    dist = lambda o: min(o[0], NY - o[0]) + min(o[1], NZ - o[1])
    return sorted(offs, key=lambda o: (-dist(o), o))


Z_FAR = (4, 3, 5, 2, 6, 1, 7)
Z_NEAR = (1, 7, 2, 6, 3, 5, 4)
Y_FAR = (2, 1, 3)


def sinkhorn_kernel(
    x_hbm, sl_hbm, sd_hbm, t_hbm, tl_hbm, td_hbm, ws_hbm, wn_hbm, cand_hbm, pp_hbm,
    out_ref,
    sl_ref, sd_ref, t_ref, tl_ref, td_ref, ws_ref, wn_ref, cand_ref, pq_ref,
    tab_ref, pp_ref, meta_ref, meta_s, acc_ref, in_sem, meta_sem,
    iota_ref, big_x, xt_ref, lk_ref, at_ref, ht_ref, tt_ref, att_ref, th_ref,
    s_ref, e_ref, wb_ref, rx_ref, rh_ref, cx_ref, top_ref, r0_ref, u_ref, sid_ref, g_ref, pk_ref,
    fs_ref, fr_ref,
    a_send, a_recv, b_send, b_recv, ya_send, ya_recv, zb_send, zb_recv, lk_send, lk_recv,
    r_send, r_recv, c_send, c_recv, f_send, f_recv,
):
    s = lax.axis_index("src")
    t = lax.axis_index("tgt")
    y = t // NZ
    z = lax.rem(t, NZ)
    tgt_peers = [lax.rem(y + dy, NY) * NZ + lax.rem(z + dz, NZ) for dy, dz in far_first()]
    sx = s // 2
    score = lax.rem(s, 2)
    src_peers = [
        lax.rem(sx + dx, 4) * 2 + (score if same else 1 - score)
        for dx, same in ((2, False), (2, True), (1, False), (3, False), (1, True), (3, True), (0, False))
    ]

    staged = (
        (sl_hbm, sl_ref), (sd_hbm, sd_ref), (cand_hbm, cand_ref), (tl_hbm, tl_ref), (td_hbm, td_ref),
        (t_hbm, t_ref), (ws_hbm, ws_ref), (wn_hbm, wn_ref), (pp_hbm, pq_ref),
        (x_hbm, big_x.at[pl.ds(t * ROWS, ROWS)]),
    )
    loads = [pltpu.make_async_copy(src, dst, in_sem.at[i]) for i, (src, dst) in enumerate(staged)]
    for load in loads:
        load.start()

    barrier = pltpu.get_barrier_semaphore()
    for p in tgt_peers:
        pl.semaphore_signal(barrier, inc=1, device_id=(s, p), device_id_type=MESH)
    for p in src_peers:
        pl.semaphore_signal(barrier, inc=1, device_id=(p, t), device_id_type=MESH)

    tile_rows = lax.broadcasted_iota(jnp.int32, (WIDE // 16, 16, BLK), 0) * 16
    tile_rows = tile_rows + lax.broadcasted_iota(jnp.int32, (WIDE // 16, 16, BLK), 1)
    iota_ref[...] = tile_rows.astype(jnp.int16)
    lane4 = lax.broadcasted_iota(jnp.int32, (KMAX // 2, BLK), 1)
    loads[0].wait()
    loads[1].wait()
    slot8 = lax.broadcasted_iota(jnp.int32, (KMAX, ROWS), 0)
    own = jnp.where(slot8 < sd_ref[...], sl_ref[...], -1)
    own = jnp.concatenate([own, own], axis=1)
    lk_ref[t] = jnp.where(lane4 < ROWS, own[:4], own[4:])

    loads[2].wait()
    local = cand_ref[...] - t * C_LOC
    local = jnp.concatenate([local, jnp.full((R_BLK, BLK - CAND), -1, jnp.int32)], axis=1)
    lane16 = lax.broadcasted_iota(jnp.int32, (R_BLK, BLK), 1)
    row16 = lax.broadcasted_iota(jnp.int32, (R_BLK, BLK), 0)
    hits = jnp.zeros((R_BLK, BLK), jnp.int32)
    for c in range(C_LOC):
        named = jnp.max(jnp.where(local == c, 1, 0), axis=1, keepdims=True)
        hits = jnp.where(lane16 == c, named, hits)
    before = jnp.zeros((R_BLK, BLK), jnp.int32)
    for r in range(R_BLK - 1):
        before = before + jnp.where(row16 > r, hits[r : r + 1, :], 0)
    place = jnp.where(hits > 0, lane16 * MOST + before, SLOTS)
    meta_ref[:R_BLK, :] = place
    rows_of_slot = [
        jnp.sum(
            jnp.where((hits > 0) & (before == m), row16 + 1, 0), axis=0, keepdims=True
        )
        for m in range(MOST)
    ]
    pad4 = jnp.zeros((8 - MOST, BLK), jnp.int32)
    meta_ref[R_BLK:, :] = jnp.concatenate(rows_of_slot + [pad4], axis=0) - 1
    table = jnp.full((R_BLK, BLK), -1, jnp.int32)
    for c in range(C_LOC):
        table = jnp.where(local == c, jnp.broadcast_to(place[:, c : c + 1], (R_BLK, BLK)), table)
    tab_ref[...] = table
    to_scalar = pltpu.make_async_copy(meta_ref, meta_s, meta_sem)
    to_scalar.start()

    def row_of(c, m):
        return meta_s[R_BLK + m, c]

    def row_at(c, m):
        return jnp.clip(row_of(c, m), 0, R_BLK - 1)

    g_ref[SLOTS] = jnp.zeros((QRY, BLK), F32)

    for load in loads[3:]:
        load.wait()
    for block in range(R_BLK):
        pp_ref[block] = pq_ref[:, block * BLK : (block + 1) * BLK]
    ws_t = ws_ref[...].T
    wn_t = wn_ref[...].T
    for chunk in range(4):
        tt_ref[:, chunk * WIDE : (chunk + 1) * WIDE] = t_ref[chunk * WIDE : (chunk + 1) * WIDE, :].T

    def build(links, chunks, put):
        singles = [part[k : k + 1, :] for part in links for k in range(part.shape[0])]
        rows, counts = [], []
        for part in links:
            count = jnp.zeros(part.shape, F32)
            for single in singles:
                count = count + jnp.where(part == single, 1.0, 0.0)
            counts += [
                jnp.broadcast_to(count[k : k + 1, :], (16, BLK)).astype(BF) for k in range(part.shape[0])
            ]
        for single in singles:
            rows.append(jnp.broadcast_to(single, (16, BLK)).astype(jnp.int16))

        def body(q, _):
            base = jnp.full((16, BLK), q * WIDE, jnp.int32).astype(jnp.int16)
            total = jnp.zeros((WIDE // 16, 16, BLK), BF)
            for k in range(KMAX):
                total = jnp.where((rows[k] - base)[None] == iota_ref[...], counts[k][None], total)
            put(q, total.reshape(WIDE, BLK))
            return 0

        lax.fori_loop(0, chunks, body, 0)

    def encode(table_t, adjacency, own_t, degree):
        total = jnp.dot(table_t, adjacency, preferred_element_type=F32)
        mean = (total / degree).astype(BF)
        mixed = jnp.dot(ws_t, own_t, preferred_element_type=F32) + jnp.dot(
            wn_t, mean, preferred_element_type=F32
        )
        return mixed.astype(BF)

    for chunk in range(4):
        cols = slice(chunk * WIDE, (chunk + 1) * WIDE)
        degree = td_ref[:, cols]
        slot_rows = lax.broadcasted_iota(jnp.int32, (KMAX, WIDE), 0)
        links = jnp.where(slot_rows < degree, tl_ref[:, cols], -1)
        degree = degree.astype(F32)
        for half in range(2):
            def put(q, value, half=half):
                att_ref[pl.ds(q * WIDE, WIDE), half * BLK : (half + 1) * BLK] = value

            build([links[:, half * BLK : (half + 1) * BLK]], 4, put)
        coded = encode(tt_ref[...], att_ref[...], tt_ref[:, cols], degree).T
        th_ref[2 * chunk] = coded[:BLK]
        th_ref[2 * chunk + 1] = coded[BLK:]

    pl.semaphore_wait(barrier, NTGT - 1 + NSRC - 1)

    def push(src, dst, ssem, rsem, dev):
        pltpu.make_async_remote_copy(
            src_ref=src, dst_ref=dst, send_sem=ssem, recv_sem=rsem, device_id=dev, device_id_type=MESH
        ).start()

    def drain(ref, sem):
        pltpu.make_async_copy(ref, ref, sem).wait()

    def part_a(d):
        return big_x.at[pl.ds(d * ROWS, A_ROWS)]

    def part_b(d):
        return big_x.at[pl.ds(d * ROWS + A_ROWS, B_ROWS)]

    def at_yz(dy, dz):
        return lax.rem(y + dy + NY, NY) * NZ + lax.rem(z + dz + NZ, NZ)

    for p in tgt_peers:
        push(lk_ref.at[t], lk_ref.at[t], lk_send, lk_recv, (s, p))
    for k in Z_FAR:
        push(part_a(t), part_a(t), a_send, a_recv.at[k], (s, at_yz(0, k)))
    for j in Y_FAR:
        push(part_b(t), part_b(t), b_send, b_recv.at[j], (s, at_yz(j, 0)))
    for j in Y_FAR:
        push(part_a(t), part_a(t), ya_send, ya_recv.at[j], (s, at_yz(j, 0)))
    for k in Z_FAR:
        push(part_b(t), part_b(t), zb_send, zb_recv.at[0], (s, at_yz(0, k)))

    for j in Y_FAR[::-1]:
        drain(part_b(t), b_recv.at[j])
        d = at_yz(-j, 0)
        for k in Z_FAR:
            push(part_b(d), part_b(d), zb_send, zb_recv.at[j], (s, at_yz(0, k)))
    def relay(near):
        for k in near:
            drain(part_a(t), a_recv.at[k])
            d = at_yz(0, -k)
            for j in Y_FAR:
                push(part_a(d), part_a(d), ya_send, ya_recv.at[j], (s, at_yz(j, 0)))

    relay(Z_NEAR[:4])
    drain(lk_ref.at[pl.ds(0, NTGT - 1)], lk_recv)

    def group_links(block):
        first, second = lk_ref[2 * block], lk_ref[2 * block + 1]
        return [
            jnp.where(lane4 < ROWS, first, pltpu.roll(second, ROWS, 1)),
            jnp.where(lane4 < ROWS, pltpu.roll(first, ROWS, 1), second),
        ]

    def build_pair(pair, _):
        for half in range(2):
            def put(q, value, half=half):
                at_ref[pair, pl.ds(q * WIDE, WIDE), half * BLK : (half + 1) * BLK] = value

            build(group_links(2 * pair + half), 8, put)
        return 0

    lax.fori_loop(0, 2, build_pair, 0)
    relay(Z_NEAR[4:6])
    lax.fori_loop(2, 4, build_pair, 0)
    relay(Z_NEAR[6:])
    lax.fori_loop(4, 8, build_pair, 0)

    for step, j in enumerate((0, 1, 3, 2)):
        if j:
            drain(big_x.at[pl.ds(0, NZ * A_ROWS)], ya_recv.at[j])
        drain(big_x.at[pl.ds(0, (NZ - 1) * B_ROWS)], zb_recv.at[j])
        pair_base = lax.rem(y - j + NY, NY) * 2
        for h in range(2):
            q = pair_base + h
            xt_ref[q] = big_x[pl.ds(pl.multiple_of(q * WIDE, WIDE), WIDE), :].T

        def add_pair(pair, _):
            total = None if step == 0 else acc_ref[pair]
            for h in range(2):
                q = pair_base + h
                part = jnp.dot(
                    xt_ref[q], at_ref[pair, pl.ds(pl.multiple_of(q * WIDE, WIDE), WIDE), :],
                    preferred_element_type=F32,
                )
                total = part if total is None else total + part
            if step < NY - 1:
                acc_ref[pair] = total
                return 0
            links = [
                jnp.concatenate(parts, axis=1)
                for parts in zip(group_links(2 * pair), group_links(2 * pair + 1))
            ]
            degree = sum(jnp.sum((part >= 0).astype(F32), axis=0, keepdims=True) for part in links)
            mean = (total / degree).astype(BF)
            mixed = jnp.dot(ws_t, xt_ref[pair], preferred_element_type=F32) + jnp.dot(
                wn_t, mean, preferred_element_type=F32
            )
            coded = mixed.astype(BF)
            ht_ref[2 * pair] = coded[:, :BLK]
            ht_ref[2 * pair + 1] = coded[:, BLK:]
            return 0

        lax.fori_loop(0, 8, add_pair, 0, unroll=8 if step == NY - 1 else 4)

    to_scalar.wait()
    block_id = lax.broadcasted_iota(jnp.int32, (R_BLK, BLK), 0)
    lane = lax.broadcasted_iota(jnp.int32, (BLK, BLK), 1)
    neg16 = jnp.full((R_BLK, BLK), NEG, F32)

    def score_block(c, best):
        for m in range(MOST):
            r = row_of(c, m)
            bias = jnp.where(r < 0, NEG, 0.0)
            raw = jnp.dot(th_ref[c], ht_ref[row_at(c, m)], preferred_element_type=F32)
            raw = raw * SCALE + bias
            s_ref[c * MOST + m] = raw
            best = jnp.maximum(best, jnp.where(block_id == r, jnp.max(raw, axis=0, keepdims=True), NEG))
        return best

    top = lax.fori_loop(0, C_LOC, score_block, neg16, unroll=8)
    top_ref[...] = top

    def first_rows(c, total):
        for m in range(MOST):
            r = row_of(c, m)
            high = top_ref[pl.ds(row_at(c, m), 1), :]
            part = jnp.sum(jnp.exp(s_ref[c * MOST + m] - high), axis=0, keepdims=True)
            total = total + jnp.where(block_id == r, part, 0.0)
        return total

    total = lax.fori_loop(0, C_LOC, first_rows, jnp.zeros((R_BLK, BLK), F32), unroll=8)
    rx_ref[0, t] = jnp.where(total > 0.0, top + jnp.log(total), NEG)

    def send_rows(sweep, buf, slot):
        for p in tgt_peers:
            push(buf.at[slot, t], buf.at[slot, t], r_send.at[sweep], r_recv.at[sweep], (s, p))

    def await_rows(sweep, buf, slot):
        drain(buf.at[slot, pl.ds(0, NTGT - 1)], r_recv.at[sweep])
        return buf[slot]

    def send_cols(sweep):
        for p in src_peers:
            push(cx_ref.at[sweep, s], cx_ref.at[sweep, s], c_send.at[sweep], c_recv.at[sweep], (p, t))

    def await_cols(sweep):
        drain(cx_ref.at[sweep, pl.ds(0, NSRC - 1)], c_recv.at[sweep])
        return cx_ref[sweep]

    send_rows(0, rx_ref, 0)

    def probe_slots(block, _):
        table = jnp.broadcast_to(tab_ref[pl.ds(block, 1), :], (8, BLK))
        for half in range(2):
            rows = slice(half * 8, half * 8 + 8)
            which = pp_ref[block, rows, :] // BLK
            sid_ref[block, rows, :] = jnp.take_along_axis(table, which, axis=1)
        return 0

    lax.fori_loop(0, R_BLK, probe_slots, 0)

    def pick(slot, _):
        r = row_at(slot // MOST, lax.rem(slot, MOST))
        for half in range(2):
            rows = slice(half * 8, half * 8 + 8)
            offset = lax.rem(pp_ref[r, rows, :], BLK)
            strip, inner = offset // 8, lax.rem(offset, 8)
            value = jnp.zeros((8, BLK), F32)
            for k in range(BLK // 8):
                got = jnp.take_along_axis(s_ref[slot, k * 8 : k * 8 + 8, :], inner, axis=0)
                value = jnp.where(strip == k, got, value)
            g_ref[slot, rows, :] = jnp.where(sid_ref[r, rows, :] == slot, value, 0.0)
        return 0

    lax.fori_loop(0, SLOTS, pick, 0, unroll=4)

    def merge(block, _):
        total = jnp.zeros((QRY, BLK), F32)
        for c in range(C_LOC):
            total = total + g_ref[jnp.clip(meta_s[block, c], 0, SLOTS)]
        pk_ref[block] = total
        return 0

    lax.fori_loop(0, R_BLK, merge, 0, unroll=4)

    parts = await_rows(0, rx_ref, 0)
    high = jnp.max(parts, axis=0)
    r0 = -(high + jnp.log(jnp.sum(jnp.exp(parts - high[None]), axis=0)))
    r0_ref[...] = r0

    def first_cols(c, carry):
        tops, sums = carry
        shifted = [
            s_ref[c * MOST + m] + r0_ref[pl.ds(row_at(c, m), 1), :]
            for m in range(MOST)
        ]
        high = functools.reduce(jnp.maximum, shifted)
        high = jnp.maximum(jnp.max(high, axis=1, keepdims=True), FLOOR)
        total = jnp.zeros((BLK, BLK), F32)
        for m in range(MOST):
            e = jnp.exp(shifted[m] - high)
            e_ref[c * MOST + m] = e
            total = total + e
        total = jnp.sum(total, axis=1, keepdims=True)
        return jnp.where(lane == c, high, tops), jnp.where(lane == c, total, sums)

    zero_tile = jnp.zeros((BLK, BLK), F32)
    tops, sums = lax.fori_loop(0, C_LOC, first_cols, (zero_tile, zero_tile), unroll=4)
    tops = tops.T[:C_LOC]
    sums = sums.T[:C_LOC]
    cx_ref[0, s] = jnp.where(sums > 0.0, tops + jnp.log(sums), NEG)
    send_cols(0)
    parts = await_cols(0)
    high = jnp.max(parts, axis=0)
    share = R_BLK * BLK * NSRC / (C_LOC * BLK * NTGT)
    c0 = math.log(share) - (high + jnp.log(jnp.sum(jnp.exp(parts - high[None]), axis=0)))
    factor = jnp.exp(tops + c0)

    def spread(weights):
        upright = jnp.concatenate([weights, jnp.zeros((BLK - C_LOC, BLK), F32)], axis=0).T
        for c in range(C_LOC):
            wb_ref[c] = jnp.broadcast_to(upright[:, c : c + 1], (BLK, BLK))

    def sweep_body(sweep, carry, rows_buf):
        _, col_scale = carry
        spread(factor * col_scale)

        def rows_of(c, total):
            for m in range(MOST):
                part = jnp.sum(e_ref[c * MOST + m] * wb_ref[c], axis=0, keepdims=True)
                total = total + jnp.where(block_id == row_of(c, m), part, 0.0)
            return total

        total = lax.fori_loop(0, C_LOC, rows_of, jnp.zeros((R_BLK, BLK), F32), unroll=8)
        slot = 1 if rows_buf is rx_ref else sweep - 1
        rows_buf[slot, t] = total.astype(rows_buf.dtype)
        send_rows(sweep, rows_buf, slot)
        parts = await_rows(sweep, rows_buf, slot)
        row_scale = 1.0 / jnp.sum(parts.astype(F32), axis=0)
        u_ref[...] = row_scale

        def cols_of(c, sums):
            total = jnp.zeros((BLK, BLK), F32)
            for m in range(MOST):
                r = row_at(c, m)
                total = total + e_ref[c * MOST + m] * u_ref[pl.ds(r, 1), :]
            return jnp.where(lane == c, jnp.sum(total, axis=1, keepdims=True), sums)

        sums = lax.fori_loop(0, C_LOC, cols_of, zero_tile, unroll=8).T[:C_LOC]
        cx_ref[sweep, s] = sums * factor
        send_cols(sweep)
        return row_scale, share / jnp.sum(await_cols(sweep), axis=0)

    scales = (jnp.ones((R_BLK, BLK), F32), jnp.ones((C_LOC, BLK), F32))
    scales = lax.fori_loop(1, SWEEPS - 1, lambda i, carry: sweep_body(i, carry, rh_ref), scales)
    row_scale, col_scale = sweep_body(SWEEPS - 1, scales, rx_ref)
    row_pot = r0 + jnp.log(row_scale)
    col_pot = c0 + jnp.log(col_scale) + math.log(CAND * BLK)
    u_ref[...] = row_pot
    top_ref[:C_LOC, :] = col_pot
    lane8 = lax.broadcasted_iota(jnp.int32, (8, BLK), 1)

    def finish(block, _):
        done = []
        for half in range(2):
            rows = slice(half * 8, half * 8 + 8)
            sid = sid_ref[block, rows, :]
            offset = lax.rem(pp_ref[block, rows, :], BLK)
            owner = sid // MOST
            value = jnp.zeros((8, BLK), F32)
            for c in range(C_LOC):
                strip = jnp.broadcast_to(top_ref[c : c + 1, :], (8, BLK))
                value = jnp.where(owner == c, jnp.take_along_axis(strip, offset, axis=1), value)
            value = value + pk_ref[block, rows, :] + u_ref[pl.ds(block, 1), :]
            done.append(jnp.where(sid >= 0, value, 0.0))
        low, high = done
        fs_ref[2 * block] = jnp.where(lane8 < ROWS, low, pltpu.roll(high, ROWS, 1))
        fs_ref[2 * block + 1] = jnp.where(lane8 < ROWS, pltpu.roll(low, ROWS, 1), high)
        return 0

    lax.fori_loop(0, R_BLK, finish, 0, unroll=8)
    for p in tgt_peers:
        push(fs_ref.at[p], fr_ref.at[t], f_send, f_recv, (s, p))
    fr_ref[t] = fs_ref[t]
    drain(big_x.at[pl.ds(0, 7 * A_ROWS)], a_send)
    drain(big_x.at[pl.ds(0, 3 * B_ROWS)], b_send)
    drain(big_x.at[pl.ds(0, 24 * A_ROWS)], ya_send)
    drain(big_x.at[pl.ds(0, 28 * B_ROWS)], zb_send)
    drain(lk_ref.at[pl.ds(0, NTGT - 1)], lk_send)
    for sweep in range(SWEEPS):
        rows_sent = rh_ref.at[sweep - 1] if 0 < sweep < SWEEPS - 1 else rx_ref.at[min(sweep, 1)]
        drain(rows_sent.at[pl.ds(0, NTGT - 1)], r_send.at[sweep])
        drain(cx_ref.at[sweep, pl.ds(0, NSRC - 1)], c_send.at[sweep])
    drain(fr_ref.at[pl.ds(0, NTGT - 1)], f_recv)
    out_ref[...] = jnp.sum(fr_ref[...], axis=0)

    drain(fs_ref.at[pl.ds(0, NTGT - 1)], f_send)


def shards(
    source_embed,
    source_links,
    source_degree,
    target_embed,
    target_links,
    target_degree,
    w_self,
    w_neigh,
    cand_blocks,
    probe_pairs,
):
    vmem = pl.BlockSpec(memory_space=pltpu.VMEM)
    hbm = pl.BlockSpec(memory_space=pltpu.HBM)
    dma = pltpu.SemaphoreType.DMA
    packed = pl.pallas_call(
        sinkhorn_kernel,
        out_shape=jax.ShapeDtypeStruct((8, BLK), F32),
        in_specs=[hbm] * 10,
        out_specs=vmem,
        scratch_shapes=[
            pltpu.VMEM((KMAX, ROWS), jnp.int32),
            pltpu.VMEM((1, ROWS), jnp.int32),
            pltpu.VMEM((C_LOC * BLK, D), BF),
            pltpu.VMEM((KMAX, C_LOC * BLK), jnp.int32),
            pltpu.VMEM((1, C_LOC * BLK), jnp.int32),
            pltpu.VMEM((D, D), BF),
            pltpu.VMEM((D, D), BF),
            pltpu.VMEM((R_BLK, CAND), jnp.int32),
            pltpu.VMEM((QRY, R_BLK * BLK), jnp.int32),
            pltpu.VMEM((R_BLK, BLK), jnp.int32),
            pltpu.VMEM((R_BLK, QRY, BLK), jnp.int32),
            pltpu.VMEM((R_BLK + 8, BLK), jnp.int32),
            pltpu.SMEM((R_BLK + 8, BLK), jnp.int32),
            pltpu.VMEM((8, D, WIDE), F32),
            dma((10,)),
            dma,
            pltpu.VMEM((WIDE // 16, 16, BLK), jnp.int16),
            pltpu.VMEM((NTGT * ROWS, D), BF),
            pltpu.VMEM((8, D, WIDE), BF),
            pltpu.VMEM((NTGT, KMAX // 2, BLK), jnp.int32),
            pltpu.VMEM((8, NTGT * ROWS, WIDE), BF),
            pltpu.VMEM((R_BLK, D, BLK), BF),
            pltpu.VMEM((D, C_LOC * BLK), BF),
            pltpu.VMEM((C_LOC * BLK, WIDE), BF),
            pltpu.VMEM((C_LOC, BLK, D), BF),
            pltpu.VMEM((SLOTS, BLK, BLK), F32),
            pltpu.VMEM((SLOTS, BLK, BLK), F32),
            pltpu.VMEM((C_LOC, BLK, BLK), F32),
            pltpu.VMEM((2, NTGT, R_BLK, BLK), F32),
            pltpu.VMEM((SWEEPS - 2, NTGT, R_BLK, BLK), BF),
            pltpu.VMEM((SWEEPS, NSRC, C_LOC, BLK), F32),
            pltpu.VMEM((R_BLK, BLK), F32),
            pltpu.VMEM((R_BLK, BLK), F32),
            pltpu.VMEM((R_BLK, BLK), F32),
            pltpu.VMEM((R_BLK, QRY, BLK), jnp.int32),
            pltpu.VMEM((SLOTS + 1, QRY, BLK), F32),
            pltpu.VMEM((R_BLK, QRY, BLK), F32),
            pltpu.VMEM((NTGT, 8, BLK), F32),
            pltpu.VMEM((NTGT, 8, BLK), F32),
            dma, dma((NZ,)), dma, dma((NY,)), dma, dma((NY,)), dma, dma((NY,)), dma, dma,
            dma((SWEEPS,)), dma((SWEEPS,)), dma((SWEEPS,)), dma((SWEEPS,)), dma, dma,
        ],
        compiler_params=pltpu.CompilerParams(
            collective_id=0, has_side_effects=True, vmem_limit_bytes=64 * 2**20
        ),
    )(
        source_embed, source_links.T, source_degree.reshape(1, -1), target_embed, target_links.T,
        target_degree.reshape(1, -1), w_self, w_neigh, cand_blocks, probe_pairs.T,
    )
    return packed.reshape(8, 2, ROWS).transpose(2, 1, 0).reshape(ROWS, QRY)


def solution(mesh):
    placed = (
        P(("src", "tgt"), None),
        P(("src", "tgt"), None),
        P(("src", "tgt")),
        P("tgt", None),
        P("tgt", None),
        P("tgt"),
        P(),
        P(),
        P("src", None),
        P("src", None),
    )
    return jax.shard_map(
        shards, mesh=mesh, in_specs=placed, out_specs=P(("src", "tgt"), None), check_vma=False
    )
```
